32 devices in a mesh: replica: 8 (over y, x, core), shard: 4 (over z).
Axes of the slice: x: 2, y: 2, z: 4, core: 2. Of those that a mesh axis runs over, the one named last changes fastest.
Arguments:
- tokens: bfloat16 [32768, 768], P(('replica', 'shard')), may hold values from -6 to 6
- cotangent: bfloat16 [32768, 768], P(('replica', 'shard')), may hold values from -6 to 6
- segments: int32 [32, 1024], P(('replica', 'shard')), may hold values from 0 to 3, never falling along the last dimension, each value on 1 to 512 neighbouring positions
- routes: int32 [32768, 1], P(('replica', 'shard')), may hold values from 0 to 3; in each aligned block of 1024 rows (0 to 1023, 1024 to 2047, ...) at most 320 rows name the same one
- w_query: bfloat16 [768, 768], P('shard'), may hold values from -0.02734375 to 0.02734375
- w_key: bfloat16 [768, 768], P('shard'), may hold values from -0.21875 to 0.21875
- w_value: bfloat16 [768, 768], P('shard'), may hold values from -0.21875 to 0.21875
- w_output: bfloat16 [768, 768], P('shard'), may hold values from -1.75 to 1.75
- norm_attn: bfloat16 [768], P('shard'), may hold values from 0.5 to 1.5
- norm_ffn: bfloat16 [768], P('shard'), may hold values from 0.5 to 1.5
- w_router: bfloat16 [768, 4], P('shard'), may hold values from -0.15625 to 0.15625
- rel_bias: bfloat16 [32, 12], P('shard'), may hold values from -4 to 4
- expert_input_weight: bfloat16 [4, 768, 3072], P('shard'), may hold values from -0.21875 to 0.21875
- expert_output_weight: bfloat16 [4, 3072, 768], P('shard'), may hold values from -0.4375 to 0.4375
Outputs:
- mixed: bfloat16 [32768, 768], P(('replica', 'shard'))
- grad_tokens: float32 [32768, 768], P(('replica', 'shard'))
- grad_query: float32 [768, 768], P('shard')
- grad_key: float32 [768, 768], P('shard')
- grad_value: float32 [768, 768], P('shard')
- grad_output: float32 [768, 768], P('shard')
- grad_norm_attn: float32 [768], P('shard')
- grad_norm_ffn: float32 [768], P('shard')
- grad_router: float32 [768, 4], P('shard')
- grad_rel_bias: float32 [32, 12], P('shard')
- grad_expert_in: float32 [4, 768, 3072], P('shard')
- grad_expert_out: float32 [4, 3072, 768], P('shard')
The draws below stay inside these ranges and needn't reach their ends.
Inputs may be any that keep to these rules, and one draw needn't show every extreme that they name: `segments`: within a sequence the segment numbers never fall; each of the 4 numbers covers 1 to 512 positions, and one covers exactly 512. `routes`: among the 1024 rows of one device no expert is named more than 320 times, and in some device's rows an expert is named exactly 320 times; every expert is named somewhere.
All inputs are finite; a program needn't handle non-finite values.
Results may differ from the reference program's by a relative error of at most 0.014.
Values may be sent and summed in bfloat16 or wider, within the bound.
No kernel may reach another device: no remote copies, remote signals or barrier semaphores. Data moves between devices by JAX's collectives and lax.ppermute only.
A program may use at most 320 MiB of HBM per device.

```python
import math
import jax
import jax.numpy as jnp
import numpy as np
from jax import lax

D = 768
FF = 3072
HEADS = 12
HEAD_DIM = 64
BUCKETS = 32
LEN = 1024
SEQ_DEV = 1
DOCS = 4
EXPERTS = 4
TOK_DEV = 1024
SEQUENCES = 32
TOKENS = 32768
CAP = 320
DEVICES = 32


def block_scale(own_key, shape, shards, least, largest):
    def one(position, shards_of):
        heights = jax.random.uniform(jax.random.fold_in(jax.random.fold_in(own_key, 6), position), (shards_of,), jnp.float32, least / len(shards), largest / len(shards))
        return jnp.repeat(jnp.exp(heights), shape[position] // shards_of).reshape((-1,) + (1,) * (len(shape) - position - 1))

    factor_of = one(*shards[0])
    for cut in shards[1:]:
        factor_of = factor_of * one(*cut)
    return factor_of


def profile(count, total, reach, skew):
    weights = [(1 << 20) // math.isqrt(grade ** skew) + 1 for grade in range(2, count + 1)]
    spare, counts = total - reach - (count - 1), [1] * (count - 1)
    while spare > 0:
        candidates = [i for i in range(count - 1) if counts[i] < reach]
        whole, remaining = sum([weights[i] for i in candidates]), spare
        for i in candidates:
            extra = min(reach - counts[i], max(1, remaining * weights[i] // whole), spare)
            counts[i] = counts[i] + extra
            spare = spare - extra
    return np.array([reach] + counts)


def ragged_sizes(rng, amount, total, most, skew):
    if amount == 2:
        one = jax.random.randint(rng, (), max(1, total - most), min(most, total - 1) + 1)
        return jnp.stack([one, total - one])
    tallies = jnp.asarray(profile(amount, total, most, skew), jnp.int32)
    pairs = (amount - 1) // 2
    source_of, sink = tallies[1:1 + 2 * pairs:2], tallies[2:2 + 2 * pairs:2]
    room = jnp.minimum(source_of - 1, most - sink)
    passed = jax.random.randint(jax.random.fold_in(rng, 1), (pairs,), 0, 1 << 20) % (room + 1)
    tallies = tallies.at[1:1 + 2 * pairs:2].set(source_of - passed).at[2:2 + 2 * pairs:2].set(sink + passed)
    return tallies[jax.random.permutation(jax.random.fold_in(rng, 2), amount)]


def assign_block(own_key, own, number, rows, count, top, bound, slope):
    ranking = jax.random.permutation(own_key, count)
    heavy_load, usual = portions_of(count, rows * top, bound, slope, True), portions_of(count, rows * top, bound, slope, False)
    places = jnp.arange(count)

    def named(tallies, turn):
        used = int((tallies > 0).sum())
        fixed = max(1, used // 4)
        passed = fixed + (places - fixed + turn * (used - fixed)) % max(1, count - fixed)
        return jnp.zeros((count,), jnp.int32).at[ranking[jnp.where(places < fixed, places, passed)]].set(jnp.asarray(tallies, jnp.int32))

    tallies = jnp.where(number % 4 == 0, named(heavy_load, number // 4), named(usual, number - number // 4 - 1))
    mixed = jax.random.permutation(jax.random.fold_in(own, 3), count)
    donor, taker = mixed[0:count // 2 * 2:2], mixed[1:count // 2 * 2:2]
    room = jnp.minimum(tallies[donor] - 1, bound - tallies[taker]) // 2
    room = jnp.where((donor == ranking[0]) | (taker == ranking[0]) | (tallies[taker] == 0), 0, jnp.maximum(room, 0))
    passed = jax.random.randint(jax.random.fold_in(own, 4), (count // 2,), 0, 1 << 20) % (room + 1)
    tallies = tallies.at[donor].add(-passed).at[taker].add(passed)
    items = jnp.searchsorted(jnp.cumsum(tallies), jnp.arange(rows * top), side="right").astype(jnp.int32)
    grid = items.reshape(top, rows).T
    grid = grid[jax.random.permutation(jax.random.fold_in(own, 1), rows)]
    turn = jax.random.randint(jax.random.fold_in(own, 2), (rows, 1), 0, top)
    return jnp.take_along_axis(grid, (jnp.arange(top)[None, :] + turn) % top, axis=1)


def portions_of(number_of, total, most, slope, full):
    loads = [(1 << 20) // math.isqrt(standing ** slope) + 1 for standing in range(1, number_of + 1)]
    largest = most if full else min(most, max(-(-total // number_of), total * loads[0] // sum(loads)))
    least = 1 if total - largest >= number_of - 1 else 0
    holding, spare = [largest] + [least] * (number_of - 1), total - largest - least * (number_of - 1)
    while spare > 0:
        free = [i for i in range(1, number_of) if holding[i] < largest] or [i for i in range(1, number_of) if holding[i] < most]
        whole, left = sum([loads[i] for i in free]), spare
        for i in free:
            extra = min(most - holding[i], max(1, left * loads[i] // whole), spare)
            holding[i] = holding[i] + extra
            spare = spare - extra
    return np.array(holding)


def gaussian(stream_key, shape, scale, most, cuts=(), kind=jnp.bfloat16):
    drawn = scale * jax.random.normal(stream_key, shape, jnp.float32)
    if cuts:
        drawn = drawn * block_scale(stream_key, shape, cuts, -0.22, 0.18)
    return jnp.clip(drawn, -most, most).astype(kind)


def setup_inputs(seed: int = 0) -> dict:
    splits = jax.random.split(jax.random.key(seed), 15)
    tokens = gaussian(splits[0], (TOKENS, D), 1.0, 6.0, ((0, 32),))
    cotangent = gaussian(splits[1], (TOKENS, D), 1.0, 6.0, ((0, 32),))
    segments = jax.vmap(lambda own: jnp.searchsorted(jnp.cumsum(ragged_sizes(own, DOCS, LEN, LEN // 2, 0)), jnp.arange(LEN), side="right"))(jax.random.split(splits[2], SEQUENCES)).reshape((SEQUENCES, LEN)).astype(jnp.int32)
    routes_keys = jax.random.split(jax.random.fold_in(splits[3], 1), TOKENS // TOK_DEV)
    routes_turns = jax.random.permutation(jax.random.fold_in(splits[3], 3), TOKENS // TOK_DEV)
    routes = jax.vmap(lambda own, number: assign_block(jax.random.fold_in(splits[3], 2), own, number, TOK_DEV, EXPERTS, 1, CAP, 1))(routes_keys, routes_turns).reshape((TOKENS, 1))
    w_query = gaussian(splits[4], (D, D), (D * HEAD_DIM) ** -0.5, 0.02734375, ((0, 4),))
    w_key = gaussian(splits[5], (D, D), D ** -0.5, 0.21875, ((0, 4),))
    w_value = gaussian(splits[6], (D, D), D ** -0.5, 0.21875, ((0, 4),))
    w_output = gaussian(splits[7], (D, D), (max(D // 64, 1)) ** -0.5, 1.75, ((0, 4),))
    norm_attn = jnp.clip(1.0 + 0.1 * jax.random.normal(splits[8], (D,), jnp.float32), 0.5, 1.5).astype(jnp.bfloat16)
    norm_ffn = jnp.clip(1.0 + 0.1 * jax.random.normal(splits[9], (D,), jnp.float32), 0.5, 1.5).astype(jnp.bfloat16)
    w_router = gaussian(splits[10], (D, EXPERTS), (2 * D) ** -0.5, 0.15625, ((0, 4),))
    rel_bias = gaussian(splits[11], (BUCKETS, HEADS), 1.0, 4.0, ((0, 4),))
    expert_input_weight = gaussian(splits[12], (EXPERTS, D, FF), D ** -0.5, 0.21875, ((0, 4),))
    expert_output_weight = gaussian(splits[13], (EXPERTS, FF, D), (FF // 16) ** -0.5, 0.4375, ((0, 4),))
    return dict(tokens=tokens, cotangent=cotangent, segments=segments, routes=routes, w_query=w_query, w_key=w_key, w_value=w_value, w_output=w_output, norm_attn=norm_attn, norm_ffn=norm_ffn, w_router=w_router, rel_bias=rel_bias, expert_input_weight=expert_input_weight, expert_output_weight=expert_output_weight)


highest = lax.Precision.HIGHEST
far_steps = (12, 16, 23, 32, 46, 64, 91)

@jax.custom_vjp
def low(v):
    return lax.optimization_barrier(v.astype(jnp.bfloat16)).astype(jnp.float32)

@jax.custom_vjp
def low_back(v):
    return v

def low_keep(v):
    return (low(v), None)

def low_pass(kept, grad):
    return (grad,)

def back_keep(v):
    return (v, None)

def back_low(kept, grad):
    return (low(grad),)
low.defvjp(low_keep, low_pass)
low_back.defvjp(back_keep, back_low)

def bucket_table(query_pos, key_pos):
    relative = key_pos[None, :] - query_pos[:, None]
    distance = jnp.abs(relative)
    beyond = jnp.zeros_like(distance)
    for threshold in far_steps:
        beyond = beyond + (distance >= threshold).astype(jnp.int32)
    inside = jnp.where(distance < 8, distance, 8 + beyond)
    return inside + 16 * (relative > 0).astype(jnp.int32)

def rms_norm(values_in, gain_vec):
    return values_in * lax.rsqrt(lax.optimization_barrier(jnp.mean(values_in * values_in, axis=-1, keepdims=True)) + 1e-06) * gain_vec

def layer(param_set, tokens_blk, segment_rows, route_col):
    full_query, full_key, full_value, full_output, gain_one, gain_two, router, relative_bias_table, first_all, second_all = param_set
    row_count, model_width = tokens_blk.shape
    seq_count, length = segment_rows.shape
    head_count = relative_bias_table.shape[1]
    head_width = model_width // head_count
    experts = router.shape[1]
    normed_one = low(rms_norm(tokens_blk, gain_one))

    def project(weight_mat):
        product = jnp.dot(normed_one, weight_mat, precision=highest)
        return low_back(low(product)).reshape(seq_count, length, head_count, head_width)
    queries = project(full_query)
    key_rows = project(full_key)
    value_rows = project(full_value)
    raw_dot = low_back(jnp.einsum('sqhe,skhe->shqk', queries, key_rows, precision=highest))
    positions = jnp.arange(length, dtype=jnp.int32)
    bucket = bucket_table(positions, positions)
    relative_bias_term = jnp.transpose(relative_bias_table[bucket], (2, 0, 1))
    scores = raw_dot + relative_bias_term[None]
    allowed = segment_rows[:, None, :, None] == segment_rows[:, None, None, :]
    scores = jnp.where(allowed, scores, -1e+30)
    chances = low(jax.nn.softmax(scores, axis=-1))
    attended = jnp.einsum('shqk,skhe->sqhe', chances, value_rows, precision=highest)
    attended = low_back(low(attended.reshape(row_count, model_width)))
    branch = low_back(jnp.dot(attended, full_output, precision=highest))
    middle = tokens_blk + branch
    normed_two = low(rms_norm(middle, gain_two))
    gate_probs = jax.nn.softmax(jnp.dot(normed_two, router, precision=highest), axis=-1)
    chosen = (route_col == jnp.arange(experts, dtype=jnp.int32)[None, :]).astype(jnp.int32)
    chosen_gate = lax.optimization_barrier(jnp.sum(gate_probs * chosen.astype(jnp.float32), axis=-1))
    slot_index = jnp.cumsum(chosen, axis=0) - chosen
    slot_range = jnp.arange(CAP, dtype=jnp.int32)
    places = ((chosen.T[:, None, :] == 1) & (slot_index.T[:, None, :] == slot_range[None, :, None])).astype(jnp.float32)
    dispatched = low_back(jnp.einsum('ect,td->ecd', places, normed_two, precision=highest))
    before_activation = low_back(jnp.einsum('ecd,edf->ecf', dispatched, first_all, precision=highest))
    hidden = low(jax.nn.gelu(before_activation))
    expert_token_rows = low_back(low(jnp.einsum('ecf,efd->ecd', hidden, second_all, precision=highest)))
    combined = jnp.einsum('ect,ecd->td', places, expert_token_rows, precision=highest)
    return middle + chosen_gate[:, None] * combined

def reference(tokens, cotangent, segments, routes, w_query, w_key, w_value, w_output, norm_attn, norm_ffn, w_router, rel_bias, expert_input_weight, expert_output_weight):
    param_set = tuple((weight_arr.astype(jnp.float32) for weight_arr in (w_query, w_key, w_value, w_output, norm_attn, norm_ffn, w_router, rel_bias, expert_input_weight, expert_output_weight)))
    token_blocks = tokens.astype(jnp.float32).reshape(DEVICES, TOK_DEV, D)
    cot_blocks = cotangent.astype(jnp.float32).reshape(DEVICES, TOK_DEV, D)
    seg_blocks = segments.reshape(DEVICES, SEQ_DEV, LEN)
    route_blocks = routes.reshape(DEVICES, TOK_DEV, 1)

    def scan_step(running, block_item):
        tokens_blk, cot_blk, seg_blk, route_blk = block_item
        out_block, pullback = jax.vjp(lambda param_arg, token_arg: layer(param_arg, token_arg, seg_blk, route_blk), param_set, tokens_blk)
        grad_params, grad_block = pullback(cot_blk)
        return (jax.tree.map(jnp.add, running, grad_params), (out_block, grad_block))
    zero_grads = jax.tree.map(jnp.zeros_like, param_set)
    summed, (out_blocks, grad_blocks) = lax.scan(scan_step, zero_grads, (token_blocks, cot_blocks, seg_blocks, route_blocks))
    return (out_blocks.reshape(TOKENS, D).astype(jnp.bfloat16), grad_blocks.reshape(TOKENS, D), summed[0], summed[1], summed[2], summed[3], summed[4], summed[5], summed[6], summed[7], summed[8], summed[9])
```

```python
from functools import partial

import jax
import jax.numpy as jnp
from jax import lax
from jax.sharding import PartitionSpec as P

highest = lax.Precision.HIGHEST
far_steps = (12, 16, 23, 32, 46, 64, 91)


def bucket_table(query_pos, key_pos):
    relative = key_pos[None, :] - query_pos[:, None]
    distance = jnp.abs(relative)
    beyond = jnp.zeros_like(distance)
    for threshold in far_steps:
        beyond = beyond + (distance >= threshold).astype(jnp.int32)
    inside = jnp.where(distance < 8, distance, 8 + beyond)
    return inside + 16 * (relative > 0).astype(jnp.int32)


def rms_norm(values_in, gain_vec):
    return (
        values_in
        * lax.rsqrt(jnp.mean(values_in * values_in, axis=-1, keepdims=True) + 1e-06)
        * gain_vec
    )


def block_scores(queries, key_rows, relative_bias_table, slot_indicators, allowed):
    raw_dot = jnp.einsum("qhe,khe->hqk", queries, key_rows, preferred_element_type=jnp.float32)
    relative_bias_term = jnp.einsum(
        "rni,rf->fni", slot_indicators, relative_bias_table, preferred_element_type=jnp.float32
    )
    scores = raw_dot + relative_bias_term
    return jnp.where(allowed[None], scores, -1e30)


def expert_forward(rows_in, first_all, second_all):
    before_activation = jnp.einsum(
        "ecd,edf->ecf", rows_in, first_all, preferred_element_type=jnp.float32
    )
    hidden = jax.nn.gelu(before_activation).astype(jnp.bfloat16)
    result = jnp.einsum(
        "ecf,efd->ecd", hidden, second_all, preferred_element_type=jnp.float32
    ).astype(jnp.bfloat16)
    return (before_activation, hidden, result)


def expert_backward(rows_in, before_activation, hidden, grad_result, first_all, second_all):
    grad_hidden = jnp.einsum(
        "ecd,efd->ecf", grad_result, second_all, preferred_element_type=jnp.float32
    )
    grad_second = jnp.einsum(
        "ecf,ecd->efd", hidden, grad_result, preferred_element_type=jnp.float32
    )
    grad_pre = jax.vjp(jax.nn.gelu, before_activation)[1](grad_hidden)[0].astype(jnp.bfloat16)
    grad_first = jnp.einsum("ecd,ecf->edf", rows_in, grad_pre, preferred_element_type=jnp.float32)
    grad_rows = jnp.einsum(
        "ecf,edf->ecd", grad_pre, first_all, preferred_element_type=jnp.float32
    ).astype(jnp.bfloat16)
    return (grad_first, grad_second, grad_rows)


def on_device(
    tokens,
    cotangent,
    segments,
    routes,
    w_query,
    w_key,
    w_value,
    w_output,
    norm_attn,
    norm_ffn,
    w_router,
    rel_bias,
    expert_input_weight,
    expert_output_weight,
):
    gathered = (
        lax.all_gather(w_query, "shard", axis=0, tiled=True),
        lax.all_gather(w_key, "shard", axis=0, tiled=True),
        lax.all_gather(w_value, "shard", axis=0, tiled=True),
        lax.all_gather(w_output, "shard", axis=0, tiled=True),
        lax.all_gather(norm_attn, "shard", axis=0, tiled=True),
        lax.all_gather(norm_ffn, "shard", axis=0, tiled=True),
        lax.all_gather(w_router, "shard", axis=0, tiled=True),
        lax.all_gather(rel_bias, "shard", axis=0, tiled=True),
    )
    (
        full_query,
        full_key,
        full_value,
        full_output,
        gain_one,
        gain_two,
        router,
        relative_bias_table,
    ) = gathered
    seq_count, length = segments.shape
    row_count, model_width = tokens.shape
    bucket_count, head_count = relative_bias_table.shape
    head_width = model_width // head_count
    experts = router.shape[1]
    qblock = min(512, length)
    positions = jnp.arange(length, dtype=jnp.int32)
    labels = jnp.arange(bucket_count, dtype=jnp.int32)

    def block_frame(which, offset):
        query_pos = positions[offset : offset + qblock]
        matches = bucket_table(query_pos, positions)[None] == labels[:, None, None]
        segment_row = segments[which]
        allowed = segment_row[offset : offset + qblock][:, None] == segment_row[None, :]
        return (matches, allowed)

    inputs = tokens.astype(jnp.float32)
    gain_one_f = gain_one.astype(jnp.float32)
    normed_one = rms_norm(inputs, gain_one_f).astype(jnp.bfloat16)

    def project(weight_mat):
        product = jnp.dot(normed_one, weight_mat, preferred_element_type=jnp.float32)
        return product.astype(jnp.bfloat16).reshape(seq_count, length, head_count, head_width)

    queries = project(full_query)
    key_rows = project(full_key)
    value_rows = project(full_value)
    pieces = []
    log_sums = []
    which = 0
    for offset in range(0, length, qblock):
        matches, allowed = block_frame(which, offset)
        scores = block_scores(
            queries[which, offset : offset + qblock],
            key_rows[which],
            relative_bias_table,
            matches.astype(jnp.bfloat16),
            allowed,
        )
        highest_score = jnp.max(scores, axis=-1, keepdims=True)
        shifted = jnp.exp(scores - highest_score)
        denominator = jnp.sum(shifted, axis=-1, keepdims=True)
        chances = (shifted / denominator).astype(jnp.bfloat16)
        log_sums.append(highest_score + jnp.log(denominator))
        pieces.append(
            jnp.einsum(
                "hqk,khe->qhe", chances, value_rows[which], preferred_element_type=jnp.float32
            )
        )
    attended = jnp.concatenate(pieces, 0).reshape(row_count, model_width).astype(jnp.bfloat16)
    branch = jnp.dot(attended, full_output, preferred_element_type=jnp.float32)
    middle = inputs + branch
    gain_two_f = gain_two.astype(jnp.float32)
    normed_two = rms_norm(middle, gain_two_f).astype(jnp.bfloat16)
    normed_two_f = normed_two.astype(jnp.float32)
    router_f = router.astype(jnp.float32)
    logits = jnp.dot(normed_two_f, router_f, precision=highest)
    gate_probs = jax.nn.softmax(logits, axis=-1)
    chosen = (routes == jnp.arange(experts, dtype=jnp.int32)[None, :]).astype(jnp.int32)
    chosen_f = chosen.astype(jnp.float32)
    chosen_gate = jnp.sum(gate_probs * chosen_f, axis=-1)
    row_ids = jnp.arange(row_count, dtype=jnp.int32)
    earlier = (row_ids[None, :] < row_ids[:, None]).astype(jnp.bfloat16)
    slot_index = jnp.dot(
        earlier, chosen.astype(jnp.bfloat16), preferred_element_type=jnp.float32
    ).astype(jnp.int32)
    capacity = 5 * row_count // (4 * experts)
    slot_range = jnp.arange(capacity, dtype=jnp.int32)
    places = (
        (chosen.T[:, None, :] == 1) & (slot_index.T[:, None, :] == slot_range[None, :, None])
    ).astype(jnp.bfloat16)
    outgoing = jnp.einsum(
        "ect,td->ecd", places, normed_two, preferred_element_type=jnp.float32
    ).astype(jnp.bfloat16)
    arrived = lax.all_to_all(outgoing, "shard", split_axis=0, concat_axis=1, tiled=True)
    before_activation, hidden, result = expert_forward(
        arrived, expert_input_weight, expert_output_weight
    )
    returned = lax.all_to_all(result, "shard", split_axis=1, concat_axis=0, tiled=True)
    combined = jnp.einsum("ect,ecd->td", places, returned, preferred_element_type=jnp.float32)
    mixed_out = (middle + chosen_gate[:, None] * combined).astype(jnp.bfloat16)
    again = (
        lax.all_gather(w_query, "shard", axis=0, tiled=True),
        lax.all_gather(w_key, "shard", axis=0, tiled=True),
        lax.all_gather(w_value, "shard", axis=0, tiled=True),
        lax.all_gather(w_output, "shard", axis=0, tiled=True),
        lax.all_gather(norm_attn, "shard", axis=0, tiled=True),
        lax.all_gather(norm_ffn, "shard", axis=0, tiled=True),
        lax.all_gather(w_router, "shard", axis=0, tiled=True),
        lax.all_gather(rel_bias, "shard", axis=0, tiled=True),
    )
    (
        full_query,
        full_key,
        full_value,
        full_output,
        gain_one,
        gain_two,
        router,
        relative_bias_table,
    ) = again
    gain_one_f = gain_one.astype(jnp.float32)
    gain_two_f = gain_two.astype(jnp.float32)
    router_f = router.astype(jnp.float32)
    grad_final = cotangent.astype(jnp.float32)
    grad_gate = jnp.sum(grad_final * combined, axis=-1)
    scaled = (chosen_gate[:, None] * grad_final).astype(jnp.bfloat16)
    grad_slots = jnp.einsum(
        "ect,td->ecd", places, scaled, preferred_element_type=jnp.float32
    ).astype(jnp.bfloat16)
    grad_arrived = lax.all_to_all(grad_slots, "shard", split_axis=0, concat_axis=1, tiled=True)
    grad_first, grad_second, grad_rows = expert_backward(
        arrived, before_activation, hidden, grad_arrived, expert_input_weight, expert_output_weight
    )
    grad_back = lax.all_to_all(grad_rows, "shard", split_axis=1, concat_axis=0, tiled=True)
    grad_normed_two = jnp.einsum(
        "ect,ecd->td", places, grad_back, preferred_element_type=jnp.float32
    )
    grad_probs_gate = chosen_f * grad_gate[:, None]
    grad_logits = jax.vjp(partial(jax.nn.softmax, axis=-1), logits)[1](grad_probs_gate)[0]
    grad_router = jnp.dot(normed_two_f.T, grad_logits, precision=highest)
    grad_normed_two = grad_normed_two + jnp.dot(grad_logits, router_f.T, precision=highest)
    pull_two = jax.vjp(rms_norm, middle, gain_two_f)[1]
    grad_mid_norm, grad_gain_two = pull_two(grad_normed_two)
    grad_middle = grad_final + grad_mid_norm
    gradient_residual_branch = grad_middle.astype(jnp.bfloat16)
    grad_wout = jnp.einsum(
        "td,te->de", attended, gradient_residual_branch, preferred_element_type=jnp.float32
    )
    grad_attended = jnp.einsum(
        "te,de->td", gradient_residual_branch, full_output, preferred_element_type=jnp.float32
    )
    grad_attended = grad_attended.astype(jnp.bfloat16).reshape(
        seq_count, length, head_count, head_width
    )
    query_grads = []
    grad_table = jnp.zeros((bucket_count, head_count), jnp.float32)
    block_index = 0
    which = 0
    key_acc = jnp.zeros((length, head_count, head_width), jnp.float32)
    value_acc = jnp.zeros((length, head_count, head_width), jnp.float32)
    for offset in range(0, length, qblock):
        matches, allowed = block_frame(which, offset)
        query_part = queries[which, offset : offset + qblock]
        scores = block_scores(
            query_part, key_rows[which], relative_bias_table, matches.astype(jnp.bfloat16), allowed
        )
        chances = jnp.exp(scores - log_sums[block_index])
        grad_part = grad_attended[which, offset : offset + qblock]
        value_acc = value_acc + jnp.einsum(
            "hqk,qhe->khe",
            chances.astype(jnp.bfloat16),
            grad_part,
            preferred_element_type=jnp.float32,
        )
        grad_chances = jnp.einsum(
            "qhe,khe->hqk", grad_part, value_rows[which], preferred_element_type=jnp.float32
        )
        inner_sum = jnp.sum(chances * grad_chances, axis=-1, keepdims=True)
        grad_scores = chances * (grad_chances - inner_sum)
        grad_table = grad_table + jnp.einsum(
            "vsi,dsi->dv",
            grad_scores,
            matches.astype(jnp.float32),
            precision=highest,
            preferred_element_type=jnp.float32,
        )
        grad_raw = grad_scores.astype(jnp.bfloat16)
        query_grads.append(
            jnp.einsum(
                "hqk,khe->qhe", grad_raw, key_rows[which], preferred_element_type=jnp.float32
            )
        )
        key_acc = key_acc + jnp.einsum(
            "hqk,qhe->khe", grad_raw, query_part, preferred_element_type=jnp.float32
        )
        block_index = block_index + 1
    key_grads = [key_acc]
    value_grads = [value_acc]
    grad_q = jnp.concatenate(query_grads, 0).reshape(row_count, model_width).astype(jnp.bfloat16)
    grad_k = jnp.stack(key_grads).reshape(row_count, model_width).astype(jnp.bfloat16)
    grad_v = jnp.stack(value_grads).reshape(row_count, model_width).astype(jnp.bfloat16)
    grad_wq = jnp.einsum("td,te->de", normed_one, grad_q, preferred_element_type=jnp.float32)
    grad_wk = jnp.einsum("td,te->de", normed_one, grad_k, preferred_element_type=jnp.float32)
    grad_wv = jnp.einsum("td,te->de", normed_one, grad_v, preferred_element_type=jnp.float32)
    grad_normed_one = jnp.einsum(
        "te,de->td", grad_q, full_query, preferred_element_type=jnp.float32
    )
    grad_normed_one = grad_normed_one + jnp.einsum(
        "te,de->td", grad_k, full_key, preferred_element_type=jnp.float32
    )
    grad_normed_one = grad_normed_one + jnp.einsum(
        "te,de->td", grad_v, full_value, preferred_element_type=jnp.float32
    )
    pull_one = jax.vjp(rms_norm, inputs, gain_one_f)[1]
    grad_in_norm, grad_gain_one = pull_one(grad_normed_one)
    grad_inputs = grad_middle + grad_in_norm
    owned_grads = (
        lax.psum_scatter(grad_wq, "shard", scatter_dimension=0, tiled=True),
        lax.psum_scatter(grad_wk, "shard", scatter_dimension=0, tiled=True),
        lax.psum_scatter(grad_wv, "shard", scatter_dimension=0, tiled=True),
        lax.psum_scatter(grad_wout, "shard", scatter_dimension=0, tiled=True),
        lax.psum_scatter(grad_gain_one, "shard", scatter_dimension=0, tiled=True),
        lax.psum_scatter(grad_gain_two, "shard", scatter_dimension=0, tiled=True),
        lax.psum_scatter(grad_router, "shard", scatter_dimension=0, tiled=True),
        lax.psum_scatter(grad_table, "shard", scatter_dimension=0, tiled=True),
    )
    summed_grads = lax.psum(
        (
            owned_grads[0],
            owned_grads[1],
            owned_grads[2],
            owned_grads[3],
            owned_grads[4],
            owned_grads[5],
            owned_grads[6],
            owned_grads[7],
        ),
        "replica",
    )
    replica_parts = (
        lax.psum_scatter(grad_first, "replica", scatter_dimension=2, tiled=True),
        lax.psum_scatter(grad_second, "replica", scatter_dimension=1, tiled=True),
    )
    total_first, total_second = (
        lax.all_gather(replica_parts[0], "replica", axis=2, tiled=True),
        lax.all_gather(replica_parts[1], "replica", axis=1, tiled=True),
    )
    return (
        mixed_out,
        grad_inputs,
        summed_grads[0],
        summed_grads[1],
        summed_grads[2],
        summed_grads[3],
        summed_grads[4],
        summed_grads[5],
        summed_grads[6],
        summed_grads[7],
        total_first,
        total_second,
    )


def solution(mesh):
    placed = (
        P(("replica", "shard"), None),
        P(("replica", "shard"), None),
        P(("replica", "shard"), None),
        P(("replica", "shard"), None),
        P("shard", None),
        P("shard", None),
        P("shard", None),
        P("shard", None),
        P("shard"),
        P("shard"),
        P("shard", None),
        P("shard", None),
        P("shard", None, None),
        P("shard", None, None),
    )
    return jax.shard_map(
        on_device,
        mesh=mesh,
        in_specs=placed,
        out_specs=(
            P(("replica", "shard"), None),
            P(("replica", "shard"), None),
            P("shard", None),
            P("shard", None),
            P("shard", None),
            P("shard", None),
            P("shard"),
            P("shard"),
            P("shard", None),
            P("shard", None),
            P("shard", None, None),
            P("shard", None, None),
        ),
        check_vma=False,
    )
```

```python
from functools import partial
import jax, jax.numpy as jnp
from jax import lax
from jax.experimental import pallas as pl
from jax.experimental.pallas import tpu as pltpu
from jax.sharding import PartitionSpec as P

f32, bf16 = jnp.float32, jnp.bfloat16
NN = (((1,), (0,)), ((), ()))
NT = (((1,), (1,)), ((), ()))
TN = (((0,), (0,)), ((), ()))
ROOT = 0.7978845608028654
CUBE = 0.044715


def dot(a, b, dims=NN):
    return lax.dot_general(a, b, dims, preferred_element_type=f32)


def attend_kernel(q_ref, k_ref, v_ref, aug_q_ref, aug_k_ref, line_ref, e_ref, att_ref, inv_ref, s_ref, k_nat, rows=256, cols=256):
    length = k_ref.shape[-1]
    band = 128
    k_nat[...] = jnp.concatenate([k_ref[0], aug_k_ref[...]], axis=0).T
    q_aug = jnp.concatenate([q_ref[0], aug_q_ref[0]], axis=0)
    v_aug = jnp.concatenate([v_ref[0], jnp.ones((16, length), bf16)], axis=0)
    line = jnp.broadcast_to(line_ref[0, 0:1, :], (band, 4 * band))
    skew = pltpu.roll(line, 0, 1, stride=1, stride_axis=0)
    near = [skew[:, (2 - o) * band : (3 - o) * band] for o in (-1, 0, 1)]
    width = v_ref.shape[1]
    for c in range(0, length, cols):
        top = None
        for r in range(0, length, rows):
            s = dot(k_nat[r : r + rows, :], q_aug[:, c : c + cols])
            pieces = []
            for i in range(r // band, (r + rows) // band):
                blocks = []
                for j in range(c // band, (c + cols) // band):
                    blk = s[i * band - r : (i + 1) * band - r, j * band - c : (j + 1) * band - c]
                    if abs(i - j) <= 1:
                        blk = blk + near[i - j + 1]
                    blocks.append(blk)
                pieces.append(jnp.concatenate(blocks, axis=1))
            s = jnp.concatenate(pieces, axis=0)
            s_ref[r : r + rows, :] = s
            m = jnp.max(s.reshape(rows // 8, 8, cols), axis=0)
            top = m if top is None else jnp.maximum(top, m)
        top = jnp.max(top, axis=0, keepdims=True)
        out = None
        for r in range(0, length, rows):
            e = jnp.exp(s_ref[r : r + rows, :] - top).astype(bf16)
            e_ref[0, r : r + rows, c : c + cols] = e
            part = dot(v_aug[:, r : r + rows], e)
            out = part if out is None else out + part
        inv = 1.0 / out[width : width + 1, :]
        inv_ref[0, :, c : c + cols] = jnp.broadcast_to(inv, (8, cols))
        att_ref[0, :, c : c + cols] = (out[:width] * inv).astype(bf16)


def attend(qkv, aug_q, aug_k, line, heads):
    width, length = qkv.shape[1:]
    head = lambda off: pl.BlockSpec((1, width, length), lambda h: (h + off, 0, 0))
    return pl.pallas_call(
        attend_kernel,
        grid=(heads,),
        in_specs=[head(0), head(heads), head(2 * heads),
                  pl.BlockSpec((1, 16, length), lambda h: (h, 0, 0)),
                  pl.BlockSpec((16, length), lambda h: (0, 0)),
                  pl.BlockSpec((1, 8, 512), lambda h: (h, 0, 0))],
        out_specs=[pl.BlockSpec((1, length, length), lambda h: (h, 0, 0)),
                   pl.BlockSpec((1, width, length), lambda h: (h, 0, 0)),
                   pl.BlockSpec((1, 8, length), lambda h: (h, 0, 0))],
        out_shape=[jax.ShapeDtypeStruct((heads, length, length), bf16),
                   jax.ShapeDtypeStruct((heads, width, length), bf16),
                   jax.ShapeDtypeStruct((heads, 8, length), f32)],
        scratch_shapes=[pltpu.VMEM((length, 256), f32), pltpu.VMEM((length, width + 16), bf16)],
        compiler_params=pltpu.CompilerParams(vmem_limit_bytes=40 * 2**20),
        cost_estimate=pl.CostEstimate(flops=heads * length * length * 256 * 4, bytes_accessed=heads * length * length * 2, transcendentals=heads * length * length),
        name="attend",
    )(qkv, qkv, qkv, aug_q, aug_k, line)


def pull_kernel(e_ref, g_ref, att_ref, inv_ref, q_ref, k_ref, v_ref, grad_ref, diag_ref, far_ref, v_nat, gs_ref, near_ref, rows=256, cols=256):
    length = k_ref.shape[-1]
    band = 128
    g = (g_ref[0].astype(f32) * inv_ref[0, 0:1, :]).astype(bf16)
    delta = jnp.sum(g.astype(f32) * att_ref[0].astype(f32), axis=0, keepdims=True)
    hi = delta.astype(bf16)
    lo = (delta - hi.astype(f32)).astype(bf16)
    pad = jnp.concatenate([hi.astype(f32), lo.astype(f32), jnp.zeros((14, length), f32)], axis=0)
    g_aug = jnp.concatenate([g, (-pad).astype(bf16)], axis=0)
    v_nat[...] = jnp.concatenate([v_ref[0], jnp.ones((16, length), bf16)], axis=0).T
    near_ref[...] = jnp.zeros_like(near_ref)
    far = [jnp.zeros((8, band), f32), jnp.zeros((8, band), f32)]
    for c in range(0, length, cols):
        for r in range(0, length, rows):
            gp = dot(v_nat[r : r + rows, :], g_aug[:, c : c + cols])
            gs = e_ref[0, r : r + rows, c : c + cols].astype(f32) * gp
            gs_ref[r : r + rows, c : c + cols] = gs.astype(bf16)
            for i in range(r // band, (r + rows) // band):
                for j in range(c // band, (c + cols) // band):
                    blk = gs[i * band - r : (i + 1) * band - r, j * band - c : (j + 1) * band - c]
                    if abs(i - j) <= 1:
                        lane = (2 - (i - j)) * band
                        near_ref[:, lane : lane + band] += blk
                    else:
                        side = int(i > j)
                        far[side] = far[side] + jnp.sum(blk.reshape(band // 8, 8, band), axis=0)
    skew = near_ref[0:8, :]
    for a in range(8, band, 8):
        skew = skew + pltpu.roll(near_ref[a : a + 8, :], 4 * band - a, 1)
    diag_ref[0] = skew
    far_ref[0] = jnp.concatenate(far, axis=1)
    grad_ref[2, 0] = dot(g, e_ref[0], NT).astype(bf16)
    grad_ref[1, 0] = dot(q_ref[0], gs_ref[...], NT).astype(bf16)
    grad_ref[0, 0] = dot(k_ref[0], gs_ref[...]).astype(bf16)


def pull(e, g, att, inv, qkv, heads):
    width, length = qkv.shape[1:]
    head = lambda off: pl.BlockSpec((1, width, length), lambda h: (h + off, 0, 0))
    return pl.pallas_call(
        pull_kernel,
        grid=(heads,),
        in_specs=[pl.BlockSpec((1, length, length), lambda h: (h, 0, 0)), head(0), head(0),
                  pl.BlockSpec((1, 8, length), lambda h: (h, 0, 0)), head(0), head(heads), head(2 * heads)],
        out_specs=[pl.BlockSpec((3, 1, width, length), lambda h: (0, h, 0, 0)),
                   pl.BlockSpec((1, 8, 512), lambda h: (h, 0, 0)),
                   pl.BlockSpec((1, 8, 256), lambda h: (h, 0, 0))],
        out_shape=[jax.ShapeDtypeStruct((3, heads, width, length), bf16), jax.ShapeDtypeStruct((heads, 8, 512), f32), jax.ShapeDtypeStruct((heads, 8, 256), f32)],
        scratch_shapes=[pltpu.VMEM((length, width + 16), bf16), pltpu.VMEM((length, length), bf16), pltpu.VMEM((128, 512), f32)],
        compiler_params=pltpu.CompilerParams(vmem_limit_bytes=40 * 2**20),
        cost_estimate=pl.CostEstimate(flops=heads * length * length * 256 * 8, bytes_accessed=heads * length * length * 2, transcendentals=0),
        name="pull",
    )(e, g, att, inv, qkv, qkv, qkv)


def bucket_of(r):
    n = jnp.abs(r)
    far = sum((n >= t).astype(jnp.int32) for t in (12, 16, 23, 32, 46, 64, 91))
    return jnp.where(n < 8, n, 8 + far) + 16 * (r > 0)


def helpers(segments, rel_bias):
    length = segments.shape[0]
    heads = rel_bias.shape[1]
    seg = (segments[None, :] == jnp.arange(4)[:, None]).astype(f32)
    blk = jnp.arange(length) // 128
    nb = length // 128
    own = (blk[None, :] == jnp.arange(nb)[:, None]).astype(f32)
    aug_k = jnp.concatenate([seg, own, jnp.zeros((12 - nb, length), f32)], 0).astype(bf16)
    left, right = rel_bias[15], rel_bias[31]
    kb = jnp.arange(nb)[:, None]
    c = jnp.where(kb < blk[None] - 1, left[:, None, None], jnp.where(kb > blk[None] + 1, right[:, None, None], 0))
    aug_q = jnp.concatenate([jnp.broadcast_to(-1e30 * (1 - seg), (heads, 4, length)), c.astype(f32), jnp.zeros((heads, 12 - nb, length), f32)], 1).astype(bf16)
    y = jnp.arange(512)
    hot = (bucket_of(-(y - 256))[None] == jnp.arange(rel_bias.shape[0])[:, None])
    line = jnp.einsum("bh,by->hy", rel_bias, hot.astype(bf16), preferred_element_type=f32)
    return aug_q, aug_k, jnp.broadcast_to(line[:, None], (heads, 8, 512))


def table_grad(diag, far, buckets):
    place = jnp.arange(512)[None, :] - jnp.arange(8)[:, None]
    hot = bucket_of(256 - place)[None] == jnp.arange(buckets)[:, None, None]
    t = jnp.einsum("kby,hby->kh", hot.astype(f32), diag, precision=lax.Precision.HIGHEST)
    l = jnp.sum(far[:, :, :128], (1, 2)); r = jnp.sum(far[:, :, 128:], (1, 2))
    b = jnp.arange(buckets)[:, None]
    return t + jnp.where(b == 15, l, 0) + jnp.where(b == 31, r, 0)


def expert_kernel(x_ref, g_ref, first_ref, second_ref, router_ref, mine_ref, *rest, experts):
    hid_ref, pre_ref, xs_ref, gs_ref, back_ref, log_ref, acc_ref, prob_ref, dot_ref = rest[-9:]
    step, last = pl.program_id(0), pl.num_programs(0) - 1
    x, g = x_ref[...], g_ref[...]

    @pl.when(step == 0)
    def _():
        lane = lax.broadcasted_iota(jnp.int32, prob_ref.shape, 1)
        logits = jnp.where(lane < experts, dot(x, router_ref[...]), -1e30)
        shifted = jnp.exp(logits - jnp.max(logits, axis=1, keepdims=True))
        prob_ref[...] = shifted / jnp.sum(shifted, axis=1, keepdims=True)
        acc_ref[...] = jnp.zeros_like(acc_ref)
        dot_ref[...] = jnp.zeros_like(dot_ref)

    gate = jnp.sum(prob_ref[...] * mine_ref[0:1, :], axis=1, keepdims=True)
    u = dot(x, first_ref[0])
    raw = dot(g, second_ref[0], NT)
    square = u * u
    t = jnp.tanh(u * (ROOT + (ROOT * CUBE) * square))
    half = 0.5 + 0.5 * t
    hidden = (u * half).astype(bf16)
    slope = half + (0.5 * u) * (1.0 - t * t) * (ROOT + (3.0 * ROOT * CUBE) * square)
    grad = (raw * gate * slope).astype(bf16)
    hid_ref[0] = hidden
    pre_ref[0] = grad
    paired = hidden.astype(f32) * raw
    total = dot_ref[...]
    for c in range(0, paired.shape[1], 128):
        total = total + paired[:, c : c + 128]
    dot_ref[...] = total
    acc_ref[...] += dot(grad, first_ref[0], NT)

    @pl.when(step == last)
    def _():
        probs = prob_ref[...]
        pull = jnp.sum(dot_ref[...], axis=1, keepdims=True)
        coming = mine_ref[0:1, :] * pull
        grad_logits = probs * (coming - jnp.sum(probs * coming, axis=1, keepdims=True))
        log_ref[...] = grad_logits
        high = grad_logits.astype(bf16)
        low = (grad_logits - high.astype(f32)).astype(bf16)
        more = dot(high, router_ref[...], NT) + dot(low, router_ref[...], NT)
        back_ref[...] = (acc_ref[...] + more).astype(bf16)
        xs_ref[0] = x
        gs_ref[0] = (g.astype(f32) * gate).astype(bf16)


def expert_pass(turn, turns, x, g, first, second, router, mine, kept, experts):
    rows, width = x.shape
    hidden = first.shape[2]
    cut = 512 if hidden % 512 == 0 else hidden
    whole = lambda *shape: pl.BlockSpec(shape, lambda s: (0,) * len(shape))
    hold = pl.BlockSpec((1, rows, cut), lambda s: (turn, 0, s))
    row = pl.BlockSpec((1, rows, width), lambda s: (turn, 0, 0))
    struct = jax.ShapeDtypeStruct
    return pl.pallas_call(
        partial(expert_kernel, experts=experts),
        grid=(hidden // cut,),
        in_specs=[
            whole(rows, width),
            whole(rows, width),
            pl.BlockSpec((1, width, cut), lambda s: (0, 0, s)),
            pl.BlockSpec((1, cut, width), lambda s: (0, s, 0)),
            whole(width, 128),
            whole(8, 128),
        ]
        + [pl.BlockSpec(memory_space=pl.ANY)] * len(kept),
        out_specs=[hold, hold, row, row, whole(rows, width), whole(rows, 128)],
        out_shape=[
            struct((turns, rows, hidden), bf16),
            struct((turns, rows, hidden), bf16),
            struct((turns, rows, width), bf16),
            struct((turns, rows, width), bf16),
            struct((rows, width), bf16),
            struct((rows, 128), f32),
        ],
        scratch_shapes=[
            pltpu.VMEM((rows, width), f32),
            pltpu.VMEM((rows, 128), f32),
            pltpu.VMEM((rows, 128), f32),
        ],
        input_output_aliases={6 + i: i for i in range(len(kept))},
        compiler_params=pltpu.CompilerParams(vmem_limit_bytes=40 * 2**20),
        cost_estimate=pl.CostEstimate(
            flops=6 * rows * width * hidden,
            bytes_accessed=4 * width * hidden + 4 * rows * hidden,
            transcendentals=rows * hidden,
        ),
        name="expert_pass",
    )(x, g, first, second, router, mine, *kept)


def rms_norm(values_in, gain_vec):
    return (
        values_in
        * lax.rsqrt(jnp.mean(values_in * values_in, axis=-1, keepdims=True) + 1e-06)
        * gain_vec
    )


def log2(n):
    return n.bit_length() - 1


def swap(x, axis, bit):
    n = lax.axis_size(axis)
    return lax.ppermute(x, axis, [(i, i ^ (1 << bit)) for i in range(n)])


def shift(x, axis, k):
    n = lax.axis_size(axis)
    return lax.ppermute(x, axis, [(i, (i + k) % n) for i in range(n)])


def side(axis, bit):
    return (lax.axis_index(axis) >> bit) & 1


def gather_bits(x, axis, dim, order):
    bits = log2(lax.axis_size(axis))
    for bit in order:
        other = swap(x, axis, bit)
        mine = side(axis, bit) == 1
        at = dim + bits - 1 - bit
        x = jnp.concatenate([jnp.where(mine, other, x), jnp.where(mine, x, other)], axis=at)
    return x


def reduce_bits(x, axis, dim, order):
    bits = log2(lax.axis_size(axis))
    for bit in order:
        at = dim + bits - 1 - bit
        mine = side(axis, bit)
        keep = lax.dynamic_index_in_dim(x, mine, at)
        away = lax.dynamic_index_in_dim(x, 1 - mine, at)
        x = (keep.astype(f32) + swap(away, axis, bit).astype(f32)).astype(bf16)
    return x


def paths(axis):
    bits = log2(lax.axis_size(axis))
    rest = list(range(1, bits))
    return rest, rest[::-1]


def spread(x, axis, ring, order):
    n, bits, m = lax.axis_size(axis), log2(lax.axis_size(axis)), lax.axis_size(ring)
    rows = x.shape[0] // n
    piece = lax.dynamic_slice_in_dim(x, lax.axis_index(axis) * rows, rows, 0)
    around = [piece] + [shift(piece, ring, m - k) for k in range(1, m)]
    double = jnp.stack(around + around)
    start = lax.rem(m - lax.axis_index(ring), m)
    held = lax.dynamic_slice_in_dim(double, start, m, 0)
    held = held.reshape((m,) + (1,) * bits + held.shape[1:])
    held = gather_bits(held, axis, 1, order + [0])
    return held.reshape(m * x.shape[0], x.shape[1])


def collect(x, axis, ring, order):
    n, bits, m = lax.axis_size(axis), log2(lax.axis_size(axis)), lax.axis_size(ring)
    rows, columns = x.shape
    x = x.reshape((m,) + (2,) * bits + (rows // m // n, columns))
    x = reduce_bits(x, axis, 1, [0] + order)
    me = lax.axis_index(ring)
    total = lax.dynamic_index_in_dim(x, me, 0).astype(f32)
    for k in range(1, m):
        away = lax.dynamic_index_in_dim(x, lax.rem(me + k, m), 0)
        total = total + shift(away, ring, k).astype(f32)
    x = gather_bits(total.astype(bf16), axis, 1, order[::-1] + [0])
    return x.reshape(rows // m, columns)


def total_of(x, axis):
    part = lax.psum_scatter(x, axis, scatter_dimension=0, tiled=True)
    return lax.all_gather(part, axis, axis=0, tiled=True)


def on_device(
    tokens,
    cotangent,
    segments,
    routes,
    w_query,
    w_key,
    w_value,
    w_output,
    norm_attn,
    norm_ffn,
    w_router,
    rel_bias,
    expert_input_weight,
    expert_output_weight,
):
    R, S = "replica", "shard"
    one, two = paths(R)
    rows, width = tokens.shape
    heads = rel_bias.shape[1]
    head = width // heads
    experts = w_router.shape[1]
    owned = w_query.shape[0]
    near = rel_bias.shape[0]
    me = lax.axis_index(S)
    capacity = 5 * rows // (4 * experts)

    extra = jnp.zeros((owned, 128), bf16)
    extra = extra.at[:, 0].set(norm_attn).at[:, 1].set(norm_ffn)
    extra = extra.at[:, 2 : 2 + experts].set(w_router).at[0 : rel_bias.shape[0], 8 : 8 + heads].set(rel_bias)
    cut = 3 * width // 2
    packed = jnp.concatenate([w_query, w_key, w_value], axis=1)
    part_one = spread(jnp.concatenate([packed[:, :cut], extra], 1), R, S, one)
    part_two = spread(packed[:, cut:], R, S, two)
    full_qkv = jnp.concatenate([part_one[:, :cut], part_two], axis=1)
    small = part_one[:, cut:]
    full_output = spread(w_output, R, S, one)
    gain_one = small[:, 0].astype(f32)
    gain_two = small[:, 1].astype(f32)
    router = small[:, 2 : 2 + experts]
    table = small.reshape(-1, owned, 128)[:, : rel_bias.shape[0], 8 : 8 + heads].reshape(-1, heads)
    buckets = table.shape[0]

    names = lax.rem(me + jnp.arange(experts, dtype=jnp.int32), experts)
    chosen = (names[:, None] == routes[:, 0][None, :]).astype(bf16)
    ids = jnp.arange(rows, dtype=jnp.int32)
    earlier = (ids[:, None] < ids[None, :]).astype(bf16)
    slot = jnp.dot(chosen, earlier, preferred_element_type=f32).astype(jnp.int32)
    places = (
        (chosen[:, None, :] == 1)
        & (slot[:, None, :] == jnp.arange(capacity, dtype=jnp.int32)[None, :, None])
    ).astype(bf16)

    def send(values):
        out = [dot(places[k], values).astype(bf16) for k in range(experts)]
        return [out[0]] + [shift(out[k], S, k) for k in range(1, experts)]

    def take(back):
        back = [back[0]] + [shift(back[k], S, experts - k) for k in range(1, experts)]
        return dot(places.reshape(-1, rows), jnp.concatenate(back, 0), TN)

    g_rows = send(cotangent)

    inputs = tokens.astype(f32)
    normed_one = rms_norm(inputs, gain_one).astype(bf16)
    qkv = lax.dot_general(full_qkv, normed_one, (((0,), (1,)), ((), ())), preferred_element_type=f32)
    qkv = qkv.astype(bf16).reshape(3 * heads, head, rows)
    aug_q, aug_k, line = helpers(segments[0], table)
    e, att, inv = attend(qkv, aug_q, aug_k, line, heads)
    att_t = att.reshape(width, rows)
    middle = inputs + dot(att_t, full_output, TN)
    normed_two = rms_norm(middle, gain_two).astype(bf16)
    x_rows = send(normed_two)

    logits = jnp.dot(normed_two, router, preferred_element_type=f32)
    gate_probs = jax.nn.softmax(logits, axis=-1)
    named = (routes == jnp.arange(experts, dtype=jnp.int32)[None, :]).astype(f32)
    chosen_gate = jnp.sum(gate_probs * named, axis=-1)

    router_wide = jnp.pad(router, ((0, 0), (0, 128 - experts)))
    mine = jnp.broadcast_to((jnp.arange(128) == me).astype(f32)[None], (8, 128))
    kept, backs, logs = (), [], []
    for k in range(experts):
        *kept, back, log = expert_pass(
            k, experts, x_rows[k], g_rows[k], expert_input_weight, expert_output_weight,
            router_wide, mine, kept, experts,
        )
        backs.append(back)
        logs.append(log)
    hid, pre, xs, gs = kept
    grad_normed_two = take(backs)
    hid_flat, pre_flat = hid.reshape(-1, hid.shape[2]), pre.reshape(-1, pre.shape[2])
    xs_flat, gs_flat = xs.reshape(-1, width), gs.reshape(-1, width)
    grad_second = dot(hid_flat, gs_flat, TN).astype(bf16)
    grad_first = dot(xs_flat, pre_flat, TN).astype(bf16)
    results = [dot(hid[k], expert_output_weight[0]).astype(bf16) for k in range(experts)]
    combined = take(results)
    mixed = (middle + chosen_gate[:, None] * combined).astype(bf16)
    total_second = total_of(grad_second, R)
    total_first = total_of(grad_first, R)
    grad_router = dot(xs_flat, jnp.concatenate(logs, 0).astype(bf16), TN)[:, :experts]

    grad_final = cotangent.astype(f32)
    grad_mid_norm, grad_gain_two = jax.vjp(rms_norm, middle, gain_two)[1](grad_normed_two)
    grad_middle = grad_final + grad_mid_norm
    grad_branch = grad_middle.astype(bf16)
    grad_wout = dot(att_t, grad_branch).astype(bf16)
    grad_att = dot(full_output, grad_branch, NT).astype(bf16).reshape(heads, head, rows)
    grad_qkv, diag, far = pull(e, grad_att, att, inv, qkv, heads)
    grad_qkv = grad_qkv.reshape(3 * width, rows)
    grad_table = table_grad(diag, far, buckets)
    grad_wqkv = lax.dot_general(
        normed_one, grad_qkv, (((0,), (1,)), ((), ())), preferred_element_type=f32
    ).astype(bf16)
    grad_normed_one = lax.dot_general(
        grad_qkv, full_qkv, (((0,), (1,)), ((), ())), preferred_element_type=f32
    )
    grad_in_norm, grad_gain_one = jax.vjp(rms_norm, inputs, gain_one)[1](grad_normed_one)
    grad_inputs = grad_middle + grad_in_norm

    rest = jnp.zeros((width, 128), bf16)
    rest = rest.at[:, 0].set(grad_gain_one.astype(bf16)).at[:, 1].set(grad_gain_two.astype(bf16))
    rest = rest.at[:, 2 : 2 + experts].set(grad_router.astype(bf16))
    rest = rest.reshape(-1, owned, 128).at[:, :near, 8 : 8 + heads].set(
        grad_table.astype(bf16).reshape(-1, near, heads)
    ).reshape(width, 128)
    sum_out = collect(grad_wout, R, S, one).astype(f32)
    sum_one = collect(jnp.concatenate([grad_wqkv[:, :cut], rest], 1), R, S, one).astype(f32)
    sum_two = collect(grad_wqkv[:, cut:], R, S, two).astype(f32)
    sum_rest = sum_one[:, cut:]
    return (
        mixed,
        grad_inputs,
        sum_one[:, :width],
        jnp.concatenate([sum_one[:, width:cut], sum_two[:, : 2 * width - cut]], 1),
        sum_two[:, 2 * width - cut :],
        sum_out,
        sum_rest[:, 0],
        sum_rest[:, 1],
        sum_rest[:, 2 : 2 + experts],
        sum_rest[:near, 8 : 8 + heads],
        total_first.astype(f32)[None],
        total_second.astype(f32)[None],
    )


def solution(mesh):
    rows = P(("replica", "shard"), None)
    own, vec, cube = P("shard", None), P("shard"), P("shard", None, None)
    return jax.shard_map(
        on_device,
        mesh=mesh,
        in_specs=(rows,) * 4 + (own,) * 4 + (vec,) * 2 + (own,) * 2 + (cube,) * 2,
        out_specs=(rows,) * 2 + (own,) * 4 + (vec,) * 2 + (own,) * 2 + (cube,) * 2,
        check_vma=False,
    )
```

```python
from functools import partial
import jax, jax.numpy as jnp
from jax import lax
from jax.experimental import pallas as pl
from jax.experimental.pallas import tpu as pltpu
from jax.sharding import PartitionSpec as P

f32, bf16 = jnp.float32, jnp.bfloat16
NN = (((1,), (0,)), ((), ()))
NT = (((1,), (1,)), ((), ()))
TN = (((0,), (0,)), ((), ()))
ROOT = 0.7978845608028654
CUBE = 0.044715


def dot(a, b, dims=NN):
    return lax.dot_general(a, b, dims, preferred_element_type=f32)


def attend_kernel(q_ref, k_ref, v_ref, aug_q_ref, aug_k_ref, line_ref, e_ref, att_ref, inv_ref, s_ref, k_nat, rows=256, cols=256):
    length = k_ref.shape[-1]
    band = 128
    k_nat[...] = jnp.concatenate([k_ref[0], aug_k_ref[...]], axis=0).T
    q_aug = jnp.concatenate([q_ref[0], aug_q_ref[0]], axis=0)
    v_aug = jnp.concatenate([v_ref[0], jnp.ones((16, length), bf16)], axis=0)
    line = jnp.broadcast_to(line_ref[0, 0:1, :], (band, 4 * band))
    skew = pltpu.roll(line, 0, 1, stride=1, stride_axis=0)
    near = [skew[:, (2 - o) * band : (3 - o) * band] for o in (-1, 0, 1)]
    width = v_ref.shape[1]
    for c in range(0, length, cols):
        top = None
        for r in range(0, length, rows):
            s = dot(k_nat[r : r + rows, :], q_aug[:, c : c + cols])
            pieces = []
            for i in range(r // band, (r + rows) // band):
                blocks = []
                for j in range(c // band, (c + cols) // band):
                    blk = s[i * band - r : (i + 1) * band - r, j * band - c : (j + 1) * band - c]
                    if abs(i - j) <= 1:
                        blk = blk + near[i - j + 1]
                    blocks.append(blk)
                pieces.append(jnp.concatenate(blocks, axis=1))
            s = jnp.concatenate(pieces, axis=0)
            s_ref[r : r + rows, :] = s
            m = jnp.max(s.reshape(rows // 8, 8, cols), axis=0)
            top = m if top is None else jnp.maximum(top, m)
        top = jnp.max(top, axis=0, keepdims=True)
        out = None
        for r in range(0, length, rows):
            e = jnp.exp(s_ref[r : r + rows, :] - top).astype(bf16)
            e_ref[0, r : r + rows, c : c + cols] = e
            part = dot(v_aug[:, r : r + rows], e)
            out = part if out is None else out + part
        inv = 1.0 / out[width : width + 1, :]
        inv_ref[0, :, c : c + cols] = jnp.broadcast_to(inv, (8, cols))
        att_ref[0, :, c : c + cols] = (out[:width] * inv).astype(bf16)


def attend(qkv, aug_q, aug_k, line, heads):
    width, length = qkv.shape[1:]
    head = lambda off: pl.BlockSpec((1, width, length), lambda h: (h + off, 0, 0))
    return pl.pallas_call(
        attend_kernel,
        grid=(heads,),
        in_specs=[head(0), head(heads), head(2 * heads),
                  pl.BlockSpec((1, 16, length), lambda h: (h, 0, 0)),
                  pl.BlockSpec((16, length), lambda h: (0, 0)),
                  pl.BlockSpec((1, 8, 512), lambda h: (h, 0, 0))],
        out_specs=[pl.BlockSpec((1, length, length), lambda h: (h, 0, 0)),
                   pl.BlockSpec((1, width, length), lambda h: (h, 0, 0)),
                   pl.BlockSpec((1, 8, length), lambda h: (h, 0, 0))],
        out_shape=[jax.ShapeDtypeStruct((heads, length, length), bf16),
                   jax.ShapeDtypeStruct((heads, width, length), bf16),
                   jax.ShapeDtypeStruct((heads, 8, length), f32)],
        scratch_shapes=[pltpu.VMEM((length, 256), f32), pltpu.VMEM((length, width + 16), bf16)],
        compiler_params=pltpu.CompilerParams(vmem_limit_bytes=40 * 2**20),
        cost_estimate=pl.CostEstimate(flops=heads * length * length * 256 * 4, bytes_accessed=heads * length * length * 2, transcendentals=heads * length * length),
        name="attend",
    )(qkv, qkv, qkv, aug_q, aug_k, line)


def pull_kernel(e_ref, g_ref, att_ref, inv_ref, q_ref, k_ref, v_ref, grad_ref, diag_ref, far_ref, v_nat, gs_ref, near_ref, rows=256, cols=256):
    length = k_ref.shape[-1]
    band = 128
    g = (g_ref[0].astype(f32) * inv_ref[0, 0:1, :]).astype(bf16)
    delta = jnp.sum(g.astype(f32) * att_ref[0].astype(f32), axis=0, keepdims=True)
    hi = delta.astype(bf16)
    lo = (delta - hi.astype(f32)).astype(bf16)
    pad = jnp.concatenate([hi.astype(f32), lo.astype(f32), jnp.zeros((14, length), f32)], axis=0)
    g_aug = jnp.concatenate([g, (-pad).astype(bf16)], axis=0)
    v_nat[...] = jnp.concatenate([v_ref[0], jnp.ones((16, length), bf16)], axis=0).T
    near_ref[...] = jnp.zeros_like(near_ref)
    far = [jnp.zeros((8, band), f32), jnp.zeros((8, band), f32)]
    for c in range(0, length, cols):
        for r in range(0, length, rows):
            gp = dot(v_nat[r : r + rows, :], g_aug[:, c : c + cols])
            gs = e_ref[0, r : r + rows, c : c + cols].astype(f32) * gp
            gs_ref[r : r + rows, c : c + cols] = gs.astype(bf16)
            for i in range(r // band, (r + rows) // band):
                for j in range(c // band, (c + cols) // band):
                    blk = gs[i * band - r : (i + 1) * band - r, j * band - c : (j + 1) * band - c]
                    if abs(i - j) <= 1:
                        lane = (2 - (i - j)) * band
                        near_ref[:, lane : lane + band] += blk
                    else:
                        side = int(i > j)
                        far[side] = far[side] + jnp.sum(blk.reshape(band // 8, 8, band), axis=0)
    skew = near_ref[0:8, :]
    for a in range(8, band, 8):
        skew = skew + pltpu.roll(near_ref[a : a + 8, :], 4 * band - a, 1)
    diag_ref[0] = skew
    far_ref[0] = jnp.concatenate(far, axis=1)
    grad_ref[2, 0] = dot(g, e_ref[0], NT).astype(bf16)
    grad_ref[1, 0] = dot(q_ref[0], gs_ref[...], NT).astype(bf16)
    grad_ref[0, 0] = dot(k_ref[0], gs_ref[...]).astype(bf16)


def pull(e, g, att, inv, qkv, heads):
    width, length = qkv.shape[1:]
    head = lambda off: pl.BlockSpec((1, width, length), lambda h: (h + off, 0, 0))
    return pl.pallas_call(
        pull_kernel,
        grid=(heads,),
        in_specs=[pl.BlockSpec((1, length, length), lambda h: (h, 0, 0)), head(0), head(0),
                  pl.BlockSpec((1, 8, length), lambda h: (h, 0, 0)), head(0), head(heads), head(2 * heads)],
        out_specs=[pl.BlockSpec((3, 1, width, length), lambda h: (0, h, 0, 0)),
                   pl.BlockSpec((1, 8, 512), lambda h: (h, 0, 0)),
                   pl.BlockSpec((1, 8, 256), lambda h: (h, 0, 0))],
        out_shape=[jax.ShapeDtypeStruct((3, heads, width, length), bf16), jax.ShapeDtypeStruct((heads, 8, 512), f32), jax.ShapeDtypeStruct((heads, 8, 256), f32)],
        scratch_shapes=[pltpu.VMEM((length, width + 16), bf16), pltpu.VMEM((length, length), bf16), pltpu.VMEM((128, 512), f32)],
        compiler_params=pltpu.CompilerParams(vmem_limit_bytes=40 * 2**20),
        cost_estimate=pl.CostEstimate(flops=heads * length * length * 256 * 8, bytes_accessed=heads * length * length * 2, transcendentals=0),
        name="pull",
    )(e, g, att, inv, qkv, qkv, qkv)


def bucket_of(r):
    n = jnp.abs(r)
    far = sum((n >= t).astype(jnp.int32) for t in (12, 16, 23, 32, 46, 64, 91))
    return jnp.where(n < 8, n, 8 + far) + 16 * (r > 0)


def helpers(segments, rel_bias):
    length = segments.shape[0]
    heads = rel_bias.shape[1]
    seg = (segments[None, :] == jnp.arange(4)[:, None]).astype(f32)
    blk = jnp.arange(length) // 128
    nb = length // 128
    own = (blk[None, :] == jnp.arange(nb)[:, None]).astype(f32)
    aug_k = jnp.concatenate([seg, own, jnp.zeros((12 - nb, length), f32)], 0).astype(bf16)
    left, right = rel_bias[15], rel_bias[31]
    kb = jnp.arange(nb)[:, None]
    c = jnp.where(kb < blk[None] - 1, left[:, None, None], jnp.where(kb > blk[None] + 1, right[:, None, None], 0))
    aug_q = jnp.concatenate([jnp.broadcast_to(-1e30 * (1 - seg), (heads, 4, length)), c.astype(f32), jnp.zeros((heads, 12 - nb, length), f32)], 1).astype(bf16)
    y = jnp.arange(512)
    hot = (bucket_of(-(y - 256))[None] == jnp.arange(rel_bias.shape[0])[:, None])
    line = jnp.einsum("bh,by->hy", rel_bias, hot.astype(bf16), preferred_element_type=f32)
    return aug_q, aug_k, jnp.broadcast_to(line[:, None], (heads, 8, 512))


def table_grad(diag, far, buckets):
    place = jnp.arange(512)[None, :] - jnp.arange(8)[:, None]
    hot = bucket_of(256 - place)[None] == jnp.arange(buckets)[:, None, None]
    t = jnp.einsum("kby,hby->kh", hot.astype(f32), diag, precision=lax.Precision.HIGHEST)
    l = jnp.sum(far[:, :, :128], (1, 2)); r = jnp.sum(far[:, :, 128:], (1, 2))
    b = jnp.arange(buckets)[:, None]
    return t + jnp.where(b == 15, l, 0) + jnp.where(b == 31, r, 0)


def expert_kernel(x_ref, g_ref, first_ref, second_ref, router_ref, mine_ref, *rest, experts):
    hid_ref, pre_ref, xs_ref, gs_ref, back_ref, log_ref, acc_ref, prob_ref, dot_ref = rest[-9:]
    step, last = pl.program_id(0), pl.num_programs(0) - 1
    x, g = x_ref[...], g_ref[...]

    @pl.when(step == 0)
    def _():
        lane = lax.broadcasted_iota(jnp.int32, prob_ref.shape, 1)
        logits = jnp.where(lane < experts, dot(x, router_ref[...]), -1e30)
        shifted = jnp.exp(logits - jnp.max(logits, axis=1, keepdims=True))
        prob_ref[...] = shifted / jnp.sum(shifted, axis=1, keepdims=True)
        acc_ref[...] = jnp.zeros_like(acc_ref)
        dot_ref[...] = jnp.zeros_like(dot_ref)

    gate = jnp.sum(prob_ref[...] * mine_ref[0:1, :], axis=1, keepdims=True)
    u = dot(x, first_ref[0])
    raw = dot(g, second_ref[0], NT)
    square = u * u
    t = jnp.tanh(u * (ROOT + (ROOT * CUBE) * square))
    half = 0.5 + 0.5 * t
    hidden = (u * half).astype(bf16)
    slope = half + (0.5 * u) * (1.0 - t * t) * (ROOT + (3.0 * ROOT * CUBE) * square)
    grad = (raw * gate * slope).astype(bf16)
    hid_ref[0] = hidden
    pre_ref[0] = grad
    paired = hidden.astype(f32) * raw
    total = dot_ref[...]
    for c in range(0, paired.shape[1], 128):
        total = total + paired[:, c : c + 128]
    dot_ref[...] = total
    acc_ref[...] += dot(grad, first_ref[0], NT)

    @pl.when(step == last)
    def _():
        probs = prob_ref[...]
        pull = jnp.sum(dot_ref[...], axis=1, keepdims=True)
        coming = mine_ref[0:1, :] * pull
        grad_logits = probs * (coming - jnp.sum(probs * coming, axis=1, keepdims=True))
        log_ref[...] = grad_logits
        high = grad_logits.astype(bf16)
        low = (grad_logits - high.astype(f32)).astype(bf16)
        more = dot(high, router_ref[...], NT) + dot(low, router_ref[...], NT)
        back_ref[...] = (acc_ref[...] + more).astype(bf16)
        xs_ref[0] = x
        gs_ref[0] = (g.astype(f32) * gate).astype(bf16)


def expert_pass(turn, turns, x, g, first, second, router, mine, kept, after, experts):
    rows, width = x.shape
    hidden = first.shape[2]
    cut = 512 if hidden % 512 == 0 else hidden
    whole = lambda *shape: pl.BlockSpec(shape, lambda s: (0,) * len(shape))
    hold = pl.BlockSpec((1, rows, cut), lambda s: (turn, 0, s))
    row = pl.BlockSpec((1, rows, width), lambda s: (turn, 0, 0))
    struct = jax.ShapeDtypeStruct
    return pl.pallas_call(
        partial(expert_kernel, experts=experts),
        grid=(hidden // cut,),
        in_specs=[
            whole(rows, width),
            whole(rows, width),
            pl.BlockSpec((1, width, cut), lambda s: (0, 0, s)),
            pl.BlockSpec((1, cut, width), lambda s: (0, s, 0)),
            whole(width, 128),
            whole(8, 128),
        ]
        + [pl.BlockSpec(memory_space=pl.ANY)] * (len(kept) + len(after)),
        out_specs=[hold, hold, row, row, whole(rows, width), whole(rows, 128)],
        out_shape=[
            struct((turns, rows, hidden), bf16),
            struct((turns, rows, hidden), bf16),
            struct((turns, rows, width), bf16),
            struct((turns, rows, width), bf16),
            struct((rows, width), bf16),
            struct((rows, 128), f32),
        ],
        scratch_shapes=[
            pltpu.VMEM((rows, width), f32),
            pltpu.VMEM((rows, 128), f32),
            pltpu.VMEM((rows, 128), f32),
        ],
        input_output_aliases={6 + i: i for i in range(len(kept))},
        compiler_params=pltpu.CompilerParams(vmem_limit_bytes=40 * 2**20),
        cost_estimate=pl.CostEstimate(
            flops=6 * rows * width * hidden,
            bytes_accessed=4 * width * hidden + 4 * rows * hidden,
            transcendentals=rows * hidden,
        ),
        name="expert_pass",
    )(x, g, first, second, router, mine, *kept, *after)


def weight_half_kernel(which_ref, hid_ref, pre_ref, xs_ref, gs_ref, after_ref, out_ref):
    @pl.when(which_ref[0] == 0)
    def _():
        out_ref[0] = dot(xs_ref[...], pre_ref[...], TN).astype(bf16)

    @pl.when(which_ref[0] == 1)
    def _():
        out_ref[0] = dot(hid_ref[...], gs_ref[...], TN).astype(bf16)


def weight_half(which, hid, pre, xs, gs, after):
    width, hidden = xs.shape[2], hid.shape[2]
    hid, pre, xs, gs = (v.reshape(-1, v.shape[2]) for v in (hid, pre, xs, gs))
    rows, parts = xs.shape[0], hidden // width
    return pl.pallas_call(
        weight_half_kernel,
        grid_spec=pltpu.PrefetchScalarGridSpec(
            num_scalar_prefetch=1,
            grid=(parts,),
            in_specs=[
                pl.BlockSpec((rows, width), lambda s, w: (0, s * w[0])),
                pl.BlockSpec((rows, width), lambda s, w: (0, s * (1 - w[0]))),
                pl.BlockSpec((rows, width), lambda s, w: (0, 0)),
                pl.BlockSpec((rows, width), lambda s, w: (0, 0)),
                pl.BlockSpec(memory_space=pl.ANY),
            ],
            out_specs=pl.BlockSpec((1, width, width), lambda s, w: (s, 0, 0)),
        ),
        out_shape=jax.ShapeDtypeStruct((parts, width, width), bf16),
        compiler_params=pltpu.CompilerParams(vmem_limit_bytes=40 * 2**20),
        cost_estimate=pl.CostEstimate(flops=2 * rows * width * hidden, bytes_accessed=2 * (rows + width) * hidden, transcendentals=0),
        name="weight_half",
    )(which.reshape(1), hid, pre, xs, gs, after)


def result_kernel(hid_ref, second_ref, after_ref, out_ref):
    out_ref[...] = dot(hid_ref[0], second_ref[0]).astype(bf16)


def result_rows(turn, hid, second, after):
    rows, hidden, width = hid.shape[1], hid.shape[2], second.shape[2]
    return pl.pallas_call(
        result_kernel,
        grid=(1,),
        in_specs=[
            pl.BlockSpec((1, rows, hidden), lambda s: (turn, 0, 0)),
            pl.BlockSpec((1, hidden, width), lambda s: (0, 0, 0)),
            pl.BlockSpec(memory_space=pl.ANY),
        ],
        out_specs=pl.BlockSpec((rows, width), lambda s: (0, 0)),
        out_shape=jax.ShapeDtypeStruct((rows, width), bf16),
        compiler_params=pltpu.CompilerParams(vmem_limit_bytes=40 * 2**20),
        cost_estimate=pl.CostEstimate(flops=2 * rows * width * hidden, bytes_accessed=2 * (rows + width) * hidden, transcendentals=0),
        name="result_rows",
    )(hid, second, after)


def widen_kernel(core_ref, half_ref, other_ref, first_ref, second_ref):
    half, other = half_ref[...].astype(f32), other_ref[...].astype(f32)
    swapped = core_ref[0] == 1
    first_ref[0] = jnp.where(swapped, other, half)
    second_ref[0] = jnp.where(swapped, half, other)


def widen(core, half, other):
    hidden, width = half.shape
    cut = width // 2
    rows = pl.BlockSpec((cut, width), lambda s, j, w: (2 * s + j, 0))
    return pl.pallas_call(
        widen_kernel,
        grid_spec=pltpu.PrefetchScalarGridSpec(
            num_scalar_prefetch=1,
            grid=(hidden // width, 2),
            in_specs=[rows, rows],
            out_specs=[
                pl.BlockSpec((1, cut, width), lambda s, j, w: (0, j, s)),
                pl.BlockSpec((1, cut, width), lambda s, j, w: (0, 2 * s + j, 0)),
            ],
        ),
        out_shape=[jax.ShapeDtypeStruct((1, width, hidden), f32), jax.ShapeDtypeStruct((1, hidden, width), f32)],
        compiler_params=pltpu.CompilerParams(vmem_limit_bytes=40 * 2**20),
        name="widen",
    )(core.reshape(1), half, other)


def rms_norm(values_in, gain_vec):
    return (
        values_in
        * lax.rsqrt(jnp.mean(values_in * values_in, axis=-1, keepdims=True) + 1e-06)
        * gain_vec
    )


def log2(n):
    return n.bit_length() - 1


def swap(x, axis, bit):
    n = lax.axis_size(axis)
    return lax.ppermute(x, axis, [(i, i ^ (1 << bit)) for i in range(n)])


def side(axis, bit):
    return (lax.axis_index(axis) >> bit) & 1


def gather_bits(x, axis, dim, order):
    bits = log2(lax.axis_size(axis))
    for bit in order:
        other = swap(x, axis, bit)
        mine = side(axis, bit) == 1
        at = dim + bits - 1 - bit
        x = jnp.concatenate([jnp.where(mine, other, x), jnp.where(mine, x, other)], axis=at)
    return x


def reduce_bits(x, axis, dim, order):
    bits = log2(lax.axis_size(axis))
    for bit in order:
        at = dim + bits - 1 - bit
        mine = side(axis, bit)
        keep = lax.dynamic_index_in_dim(x, mine, at)
        away = lax.dynamic_index_in_dim(x, 1 - mine, at)
        x = (keep.astype(f32) + swap(away, axis, bit).astype(f32)).astype(bf16)
    return x


def paths(axis):
    bits = log2(lax.axis_size(axis))
    rest = list(range(1, bits))
    return rest, rest[::-1]


def across(x, axis, k):
    n = lax.axis_size(axis)
    return lax.ppermute(x, axis, [(i, i ^ k) for i in range(n)])


def around(piece, ring):
    m, me = lax.axis_size(ring), lax.axis_index(ring)
    parts = [piece] + [across(piece, ring, k) for k in range(1, m)]
    for bit in range(log2(m)):
        odd = side(ring, bit) == 1
        parts = [jnp.where(odd, parts[k ^ (1 << bit)], parts[k]) for k in range(m)]
    return jnp.stack(parts)


def spread(held, axis, order):
    n, bits = lax.axis_size(axis), log2(lax.axis_size(axis))
    m, rows, columns = held.shape
    held = held.reshape((m,) + (1,) * bits + (rows, columns))
    held = gather_bits(held, axis, 1, order + [0])
    return held.reshape(m * n * rows, columns)


def collect(keep, away, rest, axis, ring):
    bits, m = log2(lax.axis_size(axis)) - 1, lax.axis_size(ring)
    rows, columns = keep.shape
    x = (keep.astype(f32) + swap(away, axis, 0).astype(f32)).astype(bf16)
    if rest is not None:
        more = (rest.astype(f32) + swap(rest, axis, 0).astype(f32)).astype(bf16)
        x = jnp.concatenate([x, more], 1)
    x = x.reshape((m, 2) + (2,) * bits + (rows // m // 2 >> bits, x.shape[1]))
    out = []
    for path, order in enumerate(paths(axis)):
        y = reduce_bits(x[:, path], axis, 1, order)
        me = lax.axis_index(ring)
        total = lax.dynamic_index_in_dim(y, me, 0).astype(f32)
        for k in range(1, m):
            total = total + across(lax.dynamic_index_in_dim(y, me ^ k, 0), ring, k).astype(f32)
        y = gather_bits(total.astype(bf16), axis, 1, order[::-1])
        out.append(y.reshape(rows // m // 2, x.shape[-1]))
    x = jnp.concatenate(out, 0)
    keep = x[:, :columns]
    return keep, swap(keep, axis, 0), x[:, columns:]


def on_device(
    tokens,
    cotangent,
    segments,
    routes,
    w_query,
    w_key,
    w_value,
    w_output,
    norm_attn,
    norm_ffn,
    w_router,
    rel_bias,
    expert_input_weight,
    expert_output_weight,
):
    R, S = "replica", "shard"
    one, two = paths(R)
    rows, width = tokens.shape
    heads = rel_bias.shape[1]
    head = width // heads
    experts = w_router.shape[1]
    owned = w_query.shape[0]
    near = rel_bias.shape[0]
    me = lax.axis_index(S)
    capacity = 5 * rows // (4 * experts)

    replica = lax.axis_index(R)
    few = owned // lax.axis_size(R)

    def mine_of(w):
        return lax.dynamic_slice_in_dim(w, replica * few, few, 0)

    blank = lambda n: jnp.zeros((few, n), bf16)
    bias_rows = mine_of(jnp.pad(rel_bias, ((0, owned - near), (0, 0))))
    extra = [mine_of(norm_attn)[:, None], mine_of(norm_ffn)[:, None], mine_of(w_router), blank(6 - experts), bias_rows, blank(120 - heads)]
    cut = 3 * width // 2
    packed = jnp.concatenate([mine_of(w_query), mine_of(w_key), mine_of(w_value)], axis=1)
    held_one = around(jnp.concatenate([packed[:, :cut]] + extra, 1), S)
    held_two = around(packed[:, cut:], S)
    full_output = lax.all_gather(mine_of(w_output), (S, R), axis=0, tiled=True)
    held_one, held_two, late = lax.optimization_barrier((held_one, held_two, cotangent))
    part_one, part_two = spread(held_one, R, one), spread(held_two, R, two)
    full_qkv = jnp.concatenate([part_one[:, :cut], part_two], axis=1)
    small = part_one[:, cut:]
    gain_one = small[:, 0].astype(f32)
    gain_two = small[:, 1].astype(f32)
    router = small[:, 2 : 2 + experts]
    table = small.reshape(-1, owned, 128)[:, : rel_bias.shape[0], 8 : 8 + heads].reshape(-1, heads)
    buckets = table.shape[0]

    names = me ^ jnp.arange(experts, dtype=jnp.int32)
    chosen = (names[:, None] == routes[:, 0][None, :]).astype(bf16)
    ids = jnp.arange(rows, dtype=jnp.int32)
    earlier = (ids[:, None] < ids[None, :]).astype(bf16)
    slot = jnp.dot(chosen, earlier, preferred_element_type=f32).astype(jnp.int32)
    places = (
        (chosen[:, None, :] == 1)
        & (slot[:, None, :] == jnp.arange(capacity, dtype=jnp.int32)[None, :, None])
    ).astype(bf16)

    def send(values):
        out = [dot(places[k], values).astype(bf16) for k in range(experts)]
        return [out[0]] + [across(out[k], S, k) for k in range(1, experts)]

    def take(back):
        return dot(places.reshape(-1, rows), jnp.concatenate(back, 0), TN)

    g_rows = send(late)

    inputs = tokens.astype(f32)
    normed_one = rms_norm(inputs, gain_one).astype(bf16)
    qkv = lax.dot_general(full_qkv, normed_one, (((0,), (1,)), ((), ())), preferred_element_type=f32)
    qkv = qkv.astype(bf16).reshape(3 * heads, head, rows)
    aug_q, aug_k, line = helpers(segments[0], table)
    e, att, inv = attend(qkv, aug_q, aug_k, line, heads)
    att_t = att.reshape(width, rows)
    middle = inputs + dot(att_t, full_output, TN)
    normed_two = rms_norm(middle, gain_two).astype(bf16)
    x_rows = send(normed_two)

    logits = jnp.dot(normed_two, router, preferred_element_type=f32)
    gate_probs = jax.nn.softmax(logits, axis=-1)
    named = (routes == jnp.arange(experts, dtype=jnp.int32)[None, :]).astype(f32)
    chosen_gate = jnp.sum(gate_probs * named, axis=-1)

    router_wide = jnp.pad(router, ((0, 0), (0, 128 - experts)))
    mine = jnp.broadcast_to((jnp.arange(128) == me).astype(f32)[None], (8, 128))
    kept, backs, logs = (), [], []
    for k in range(experts):
        *kept, back, log = expert_pass(
            k, experts, x_rows[k], g_rows[k], expert_input_weight, expert_output_weight,
            router_wide, mine, kept, backs[k - 2 : k - 1] if k > 2 else [], experts,
        )
        backs.append(across(back, S, k) if k else back)
        logs.append(log)
    hid, pre, xs, gs = kept
    core = side(R, 0)
    away = weight_half(1 - core, hid, pre, xs, gs, backs[-2])
    swapped = swap(away, R, 0)
    keep = weight_half(core, hid, pre, xs, gs, backs[-1])
    half = (keep.astype(f32) + swapped.astype(f32)).astype(bf16).reshape(-1, width)
    groups = [list(range(j, lax.axis_size(R), 2)) for j in (0, 1)]
    part = lax.psum_scatter(half, R, scatter_dimension=0, tiled=True, axis_index_groups=groups)
    half = lax.all_gather(part, R, axis=0, tiled=True, axis_index_groups=groups)
    total_first, total_second = widen(core, half, swap(half, R, 0))
    xs_flat = xs.reshape(-1, width)
    grad_normed_two = take(backs)
    grad_router = dot(xs_flat, jnp.concatenate(logs, 0).astype(bf16), TN)[:, :experts]

    grad_final = cotangent.astype(f32)
    grad_mid_norm, grad_gain_two = jax.vjp(rms_norm, middle, gain_two)[1](grad_normed_two)
    grad_middle = grad_final + grad_mid_norm
    grad_branch = grad_middle.astype(bf16)
    mid = width // 2

    def halves(make, count):
        return make(core * count), make((1 - core) * count)

    out_keep, out_away = halves(
        lambda at: dot(att_t, lax.dynamic_slice_in_dim(grad_branch, at, mid, 1)).astype(bf16), mid
    )
    grad_att = dot(full_output, grad_branch, NT).astype(bf16).reshape(heads, head, rows)
    results = [result_rows(k, hid, expert_output_weight, grad_att) for k in range(experts)]
    results = [results[0]] + [across(results[k], S, k) for k in range(1, experts)]
    mixed = (middle + chosen_gate[:, None] * take(results)).astype(bf16)
    grad_qkv, diag, far = pull(e, grad_att, att, inv, qkv, heads)
    grad_qkv = grad_qkv.reshape(3 * width, rows)
    grad_table = table_grad(diag, far, buckets)
    half_dims = (((0,), (1,)), ((), ()))
    qkv_keep, qkv_away = halves(
        lambda at: dot(normed_one, lax.dynamic_slice_in_dim(grad_qkv, at, cut, 0), half_dims).astype(bf16), cut
    )
    grad_normed_one = lax.dot_general(
        grad_qkv, full_qkv, (((0,), (1,)), ((), ())), preferred_element_type=f32
    )
    grad_in_norm, grad_gain_one = jax.vjp(rms_norm, inputs, gain_one)[1](grad_normed_one)
    grad_inputs = grad_middle + grad_in_norm

    table_rows = jnp.pad(grad_table.reshape(-1, near, heads), ((0, 0), (0, owned - near), (0, 0))).reshape(width, heads)
    rest = jnp.concatenate(
        [grad_gain_one[:, None], grad_gain_two[:, None], grad_router, jnp.zeros((width, 6 - experts), f32), table_rows, jnp.zeros((width, 120 - heads), f32)], 1
    ).astype(bf16)
    out_keep, out_away, _ = collect(out_keep, out_away, None, R, S)
    qkv_keep, qkv_away, sum_rest = collect(qkv_keep, qkv_away, rest, R, S)

    def ordered(keep, away):
        return jnp.concatenate([jnp.where(core == 0, keep, away), jnp.where(core == 0, away, keep)], 1).astype(f32)

    sum_qkv, sum_out = ordered(qkv_keep, qkv_away), ordered(out_keep, out_away)
    sum_rest = sum_rest.astype(f32)
    return (
        mixed,
        grad_inputs,
        sum_qkv[:, :width],
        sum_qkv[:, width : 2 * width],
        sum_qkv[:, 2 * width :],
        sum_out,
        sum_rest[:, 0],
        sum_rest[:, 1],
        sum_rest[:, 2 : 2 + experts],
        sum_rest[:near, 8 : 8 + heads],
        total_first,
        total_second,
    )


def solution(mesh):
    rows = P(("replica", "shard"), None)
    own, vec, cube = P("shard", None), P("shard"), P("shard", None, None)
    return jax.shard_map(
        on_device,
        mesh=mesh,
        in_specs=(rows,) * 4 + (own,) * 4 + (vec,) * 2 + (own,) * 2 + (cube,) * 2,
        out_specs=(rows,) * 2 + (own,) * 4 + (vec,) * 2 + (own,) * 2 + (cube,) * 2,
        check_vma=False,
    )
```

```python
from functools import partial
import jax, jax.numpy as jnp
from jax import lax
from jax.experimental import pallas as pl
from jax.experimental.pallas import tpu as pltpu
from jax.sharding import PartitionSpec as P

f32, bf16 = jnp.float32, jnp.bfloat16
NN = (((1,), (0,)), ((), ()))
NT = (((1,), (1,)), ((), ()))
TN = (((0,), (0,)), ((), ()))
ROOT = 0.7978845608028654
CUBE = 0.044715


def dot(a, b, dims=NN):
    return lax.dot_general(a, b, dims, preferred_element_type=f32)


def attend_kernel(q_ref, k_ref, v_ref, aug_q_ref, aug_k_ref, line_ref, e_ref, att_ref, inv_ref, s_ref, k_nat, rows=256, cols=256):
    length = k_ref.shape[-1]
    band = 128
    k_nat[...] = jnp.concatenate([k_ref[0], aug_k_ref[...]], axis=0).T
    q_aug = jnp.concatenate([q_ref[0], aug_q_ref[0]], axis=0)
    v_aug = jnp.concatenate([v_ref[0], jnp.ones((16, length), bf16)], axis=0)
    line = jnp.broadcast_to(line_ref[0, 0:1, :], (band, 4 * band))
    skew = pltpu.roll(line, 0, 1, stride=1, stride_axis=0)
    near = [skew[:, (2 - o) * band : (3 - o) * band] for o in (-1, 0, 1)]
    width = v_ref.shape[1]
    for c in range(0, length, cols):
        top = None
        for r in range(0, length, rows):
            s = dot(k_nat[r : r + rows, :], q_aug[:, c : c + cols])
            pieces = []
            for i in range(r // band, (r + rows) // band):
                blocks = []
                for j in range(c // band, (c + cols) // band):
                    blk = s[i * band - r : (i + 1) * band - r, j * band - c : (j + 1) * band - c]
                    if abs(i - j) <= 1:
                        blk = blk + near[i - j + 1]
                    blocks.append(blk)
                pieces.append(jnp.concatenate(blocks, axis=1))
            s = jnp.concatenate(pieces, axis=0)
            s_ref[r : r + rows, :] = s
            m = jnp.max(s.reshape(rows // 8, 8, cols), axis=0)
            top = m if top is None else jnp.maximum(top, m)
        top = jnp.max(top, axis=0, keepdims=True)
        out = None
        for r in range(0, length, rows):
            e = jnp.exp(s_ref[r : r + rows, :] - top).astype(bf16)
            e_ref[0, r : r + rows, c : c + cols] = e
            part = dot(v_aug[:, r : r + rows], e)
            out = part if out is None else out + part
        inv = 1.0 / out[width : width + 1, :]
        inv_ref[0, :, c : c + cols] = jnp.broadcast_to(inv, (8, cols))
        att_ref[0, :, c : c + cols] = (out[:width] * inv).astype(bf16)


def attend(qkv, aug_q, aug_k, line, heads):
    width, length = qkv.shape[1:]
    head = lambda off: pl.BlockSpec((1, width, length), lambda h: (h + off, 0, 0))
    return pl.pallas_call(
        attend_kernel,
        grid=(heads,),
        in_specs=[head(0), head(heads), head(2 * heads),
                  pl.BlockSpec((1, 16, length), lambda h: (h, 0, 0)),
                  pl.BlockSpec((16, length), lambda h: (0, 0)),
                  pl.BlockSpec((1, 8, 512), lambda h: (h, 0, 0))],
        out_specs=[pl.BlockSpec((1, length, length), lambda h: (h, 0, 0)),
                   pl.BlockSpec((1, width, length), lambda h: (h, 0, 0)),
                   pl.BlockSpec((1, 8, length), lambda h: (h, 0, 0))],
        out_shape=[jax.ShapeDtypeStruct((heads, length, length), bf16),
                   jax.ShapeDtypeStruct((heads, width, length), bf16),
                   jax.ShapeDtypeStruct((heads, 8, length), f32)],
        scratch_shapes=[pltpu.VMEM((length, 256), f32), pltpu.VMEM((length, width + 16), bf16)],
        compiler_params=pltpu.CompilerParams(vmem_limit_bytes=40 * 2**20),
        cost_estimate=pl.CostEstimate(flops=heads * length * length * 256 * 4, bytes_accessed=heads * length * length * 2, transcendentals=heads * length * length),
        name="attend",
    )(qkv, qkv, qkv, aug_q, aug_k, line)


def pull_kernel(e_ref, g_ref, att_ref, inv_ref, q_ref, k_ref, v_ref, *rest, rows=256, cols=256):
    grad_ref, diag_ref, far_ref, v_nat, gs_ref, near_ref = rest[-6:]
    length = k_ref.shape[-1]
    band = 128
    g = (g_ref[0].astype(f32) * inv_ref[0, 0:1, :]).astype(bf16)
    delta = jnp.sum(g.astype(f32) * att_ref[0].astype(f32), axis=0, keepdims=True)
    hi = delta.astype(bf16)
    lo = (delta - hi.astype(f32)).astype(bf16)
    pad = jnp.concatenate([hi.astype(f32), lo.astype(f32), jnp.zeros((14, length), f32)], axis=0)
    g_aug = jnp.concatenate([g, (-pad).astype(bf16)], axis=0)
    v_nat[...] = jnp.concatenate([v_ref[0], jnp.ones((16, length), bf16)], axis=0).T
    near_ref[...] = jnp.zeros_like(near_ref)
    far = [jnp.zeros((8, band), f32), jnp.zeros((8, band), f32)]
    for c in range(0, length, cols):
        for r in range(0, length, rows):
            gp = dot(v_nat[r : r + rows, :], g_aug[:, c : c + cols])
            gs = e_ref[0, r : r + rows, c : c + cols].astype(f32) * gp
            gs_ref[r : r + rows, c : c + cols] = gs.astype(bf16)
            for i in range(r // band, (r + rows) // band):
                for j in range(c // band, (c + cols) // band):
                    blk = gs[i * band - r : (i + 1) * band - r, j * band - c : (j + 1) * band - c]
                    if abs(i - j) <= 1:
                        lane = (2 - (i - j)) * band
                        near_ref[:, lane : lane + band] += blk
                    else:
                        side = int(i > j)
                        far[side] = far[side] + jnp.sum(blk.reshape(band // 8, 8, band), axis=0)
    skew = near_ref[0:8, :]
    for a in range(8, band, 8):
        skew = skew + pltpu.roll(near_ref[a : a + 8, :], 4 * band - a, 1)
    diag_ref[0] = skew
    far_ref[0] = jnp.concatenate(far, axis=1)
    grad_ref[2, 0] = dot(g, e_ref[0], NT).astype(bf16)
    grad_ref[1, 0] = dot(q_ref[0], gs_ref[...], NT).astype(bf16)
    grad_ref[0, 0] = dot(k_ref[0], gs_ref[...]).astype(bf16)


def pull(e, g, att, inv, qkv, heads, after):
    width, length = qkv.shape[1:]
    head = lambda off: pl.BlockSpec((1, width, length), lambda h: (h + off, 0, 0))
    return pl.pallas_call(
        pull_kernel,
        grid=(heads,),
        in_specs=[pl.BlockSpec((1, length, length), lambda h: (h, 0, 0)), head(0), head(0),
                  pl.BlockSpec((1, 8, length), lambda h: (h, 0, 0)), head(0), head(heads), head(2 * heads)]
        + [pl.BlockSpec(memory_space=pl.ANY)] * len(after),
        out_specs=[pl.BlockSpec((3, 1, width, length), lambda h: (0, h, 0, 0)),
                   pl.BlockSpec((1, 8, 512), lambda h: (h, 0, 0)),
                   pl.BlockSpec((1, 8, 256), lambda h: (h, 0, 0))],
        out_shape=[jax.ShapeDtypeStruct((3, heads, width, length), bf16), jax.ShapeDtypeStruct((heads, 8, 512), f32), jax.ShapeDtypeStruct((heads, 8, 256), f32)],
        scratch_shapes=[pltpu.VMEM((length, width + 16), bf16), pltpu.VMEM((length, length), bf16), pltpu.VMEM((128, 512), f32)],
        compiler_params=pltpu.CompilerParams(vmem_limit_bytes=40 * 2**20),
        cost_estimate=pl.CostEstimate(flops=heads * length * length * 256 * 8, bytes_accessed=heads * length * length * 2, transcendentals=0),
        name="pull",
    )(e, g, att, inv, qkv, qkv, qkv, *after)


def bucket_of(r):
    n = jnp.abs(r)
    far = sum((n >= t).astype(jnp.int32) for t in (12, 16, 23, 32, 46, 64, 91))
    return jnp.where(n < 8, n, 8 + far) + 16 * (r > 0)


def helpers(segments, rel_bias):
    length = segments.shape[0]
    heads = rel_bias.shape[1]
    seg = (segments[None, :] == jnp.arange(4)[:, None]).astype(f32)
    blk = jnp.arange(length) // 128
    nb = length // 128
    own = (blk[None, :] == jnp.arange(nb)[:, None]).astype(f32)
    aug_k = jnp.concatenate([seg, own, jnp.zeros((12 - nb, length), f32)], 0).astype(bf16)
    left, right = rel_bias[15], rel_bias[31]
    kb = jnp.arange(nb)[:, None]
    c = jnp.where(kb < blk[None] - 1, left[:, None, None], jnp.where(kb > blk[None] + 1, right[:, None, None], 0))
    aug_q = jnp.concatenate([jnp.broadcast_to(-1e30 * (1 - seg), (heads, 4, length)), c.astype(f32), jnp.zeros((heads, 12 - nb, length), f32)], 1).astype(bf16)
    y = jnp.arange(512)
    hot = (bucket_of(-(y - 256))[None] == jnp.arange(rel_bias.shape[0])[:, None])
    line = jnp.einsum("bh,by->hy", rel_bias, hot.astype(bf16), preferred_element_type=f32)
    return aug_q, aug_k, jnp.broadcast_to(line[:, None], (heads, 8, 512))


def table_grad(diag, far, buckets):
    place = jnp.arange(512)[None, :] - jnp.arange(8)[:, None]
    hot = bucket_of(256 - place)[None] == jnp.arange(buckets)[:, None, None]
    t = jnp.einsum("kby,hby->kh", hot.astype(f32), diag, precision=lax.Precision.HIGHEST)
    l = jnp.sum(far[:, :, :128], (1, 2)); r = jnp.sum(far[:, :, 128:], (1, 2))
    b = jnp.arange(buckets)[:, None]
    return t + jnp.where(b == 15, l, 0) + jnp.where(b == 31, r, 0)


def expert_kernel(x_ref, g_ref, first_ref, second_ref, router_ref, mine_ref, *rest, experts):
    hid_ref, pre_ref, xs_ref, gs_ref, back_ref, log_ref, acc_ref, prob_ref, dot_ref = rest[-9:]
    step, last = pl.program_id(0), pl.num_programs(0) - 1
    x, g = x_ref[...], g_ref[...]

    @pl.when(step == 0)
    def _():
        lane = lax.broadcasted_iota(jnp.int32, prob_ref.shape, 1)
        logits = jnp.where(lane < experts, dot(x, router_ref[...]), -1e30)
        shifted = jnp.exp(logits - jnp.max(logits, axis=1, keepdims=True))
        prob_ref[...] = shifted / jnp.sum(shifted, axis=1, keepdims=True)
        acc_ref[...] = jnp.zeros_like(acc_ref)
        dot_ref[...] = jnp.zeros_like(dot_ref)

    gate = jnp.sum(prob_ref[...] * mine_ref[0:1, :], axis=1, keepdims=True)
    u = dot(x, first_ref[0])
    raw = dot(g, second_ref[0], NT)
    square = u * u
    t = jnp.tanh(u * (ROOT + (ROOT * CUBE) * square))
    half = 0.5 + 0.5 * t
    hidden = (u * half).astype(bf16)
    slope = half + (0.5 * u) * (1.0 - t * t) * (ROOT + (3.0 * ROOT * CUBE) * square)
    grad = (raw * gate * slope).astype(bf16)
    hid_ref[0] = hidden
    pre_ref[0] = grad
    paired = hidden.astype(f32) * raw
    total = dot_ref[...]
    for c in range(0, paired.shape[1], 128):
        total = total + paired[:, c : c + 128]
    dot_ref[...] = total
    acc_ref[...] += dot(grad, first_ref[0], NT)

    @pl.when(step == last)
    def _():
        probs = prob_ref[...]
        pull = jnp.sum(dot_ref[...], axis=1, keepdims=True)
        coming = mine_ref[0:1, :] * pull
        grad_logits = probs * (coming - jnp.sum(probs * coming, axis=1, keepdims=True))
        log_ref[...] = grad_logits
        high = grad_logits.astype(bf16)
        low = (grad_logits - high.astype(f32)).astype(bf16)
        more = dot(high, router_ref[...], NT) + dot(low, router_ref[...], NT)
        back_ref[...] = (acc_ref[...] + more).astype(bf16)
        xs_ref[0] = x
        gs_ref[0] = (g.astype(f32) * gate).astype(bf16)


def expert_pass(turn, turns, x, g, first, second, router, mine, kept, after, experts):
    rows, width = x.shape
    hidden = first.shape[2]
    cut = 512 if hidden % 512 == 0 else hidden
    whole = lambda *shape: pl.BlockSpec(shape, lambda s: (0,) * len(shape))
    hold = pl.BlockSpec((1, rows, cut), lambda s: (turn, 0, s))
    row = pl.BlockSpec((1, rows, width), lambda s: (turn, 0, 0))
    struct = jax.ShapeDtypeStruct
    return pl.pallas_call(
        partial(expert_kernel, experts=experts),
        grid=(hidden // cut,),
        in_specs=[
            whole(rows, width),
            whole(rows, width),
            pl.BlockSpec((1, width, cut), lambda s: (0, 0, s)),
            pl.BlockSpec((1, cut, width), lambda s: (0, s, 0)),
            whole(width, 128),
            whole(8, 128),
        ]
        + [pl.BlockSpec(memory_space=pl.ANY)] * (len(kept) + len(after)),
        out_specs=[hold, hold, row, row, whole(rows, width), whole(rows, 128)],
        out_shape=[
            struct((turns, rows, hidden), bf16),
            struct((turns, rows, hidden), bf16),
            struct((turns, rows, width), bf16),
            struct((turns, rows, width), bf16),
            struct((rows, width), bf16),
            struct((rows, 128), f32),
        ],
        scratch_shapes=[
            pltpu.VMEM((rows, width), f32),
            pltpu.VMEM((rows, 128), f32),
            pltpu.VMEM((rows, 128), f32),
        ],
        input_output_aliases={6 + i: i for i in range(len(kept))},
        compiler_params=pltpu.CompilerParams(vmem_limit_bytes=40 * 2**20),
        cost_estimate=pl.CostEstimate(
            flops=6 * rows * width * hidden,
            bytes_accessed=4 * width * hidden + 4 * rows * hidden,
            transcendentals=rows * hidden,
        ),
        name="expert_pass",
    )(x, g, first, second, router, mine, *kept, *after)


def weight_half_kernel(which_ref, hid_ref, pre_ref, xs_ref, gs_ref, after_ref, out_ref):
    @pl.when(which_ref[0] == 0)
    def _():
        out_ref[0] = dot(xs_ref[...], pre_ref[...], TN).astype(bf16)

    @pl.when(which_ref[0] == 1)
    def _():
        out_ref[0] = dot(hid_ref[...], gs_ref[...], TN).astype(bf16)


def weight_half(which, hid, pre, xs, gs, after):
    width, hidden = xs.shape[2], hid.shape[2]
    hid, pre, xs, gs = (v.reshape(-1, v.shape[2]) for v in (hid, pre, xs, gs))
    rows, parts = xs.shape[0], hidden // width
    return pl.pallas_call(
        weight_half_kernel,
        grid_spec=pltpu.PrefetchScalarGridSpec(
            num_scalar_prefetch=1,
            grid=(parts,),
            in_specs=[
                pl.BlockSpec((rows, width), lambda s, w: (0, s * w[0])),
                pl.BlockSpec((rows, width), lambda s, w: (0, s * (1 - w[0]))),
                pl.BlockSpec((rows, width), lambda s, w: (0, 0)),
                pl.BlockSpec((rows, width), lambda s, w: (0, 0)),
                pl.BlockSpec(memory_space=pl.ANY),
            ],
            out_specs=pl.BlockSpec((1, width, width), lambda s, w: (s, 0, 0)),
        ),
        out_shape=jax.ShapeDtypeStruct((parts, width, width), bf16),
        compiler_params=pltpu.CompilerParams(vmem_limit_bytes=40 * 2**20),
        cost_estimate=pl.CostEstimate(flops=2 * rows * width * hidden, bytes_accessed=2 * (rows + width) * hidden, transcendentals=0),
        name="weight_half",
    )(which.reshape(1), hid, pre, xs, gs, after)


def result_kernel(hid_ref, second_ref, after_ref, out_ref):
    out_ref[...] = dot(hid_ref[0], second_ref[0]).astype(bf16)


def result_rows(turn, hid, second, after):
    rows, hidden, width = hid.shape[1], hid.shape[2], second.shape[2]
    return pl.pallas_call(
        result_kernel,
        grid=(1,),
        in_specs=[
            pl.BlockSpec((1, rows, hidden), lambda s: (turn, 0, 0)),
            pl.BlockSpec((1, hidden, width), lambda s: (0, 0, 0)),
            pl.BlockSpec(memory_space=pl.ANY),
        ],
        out_specs=pl.BlockSpec((rows, width), lambda s: (0, 0)),
        out_shape=jax.ShapeDtypeStruct((rows, width), bf16),
        compiler_params=pltpu.CompilerParams(vmem_limit_bytes=40 * 2**20),
        cost_estimate=pl.CostEstimate(flops=2 * rows * width * hidden, bytes_accessed=2 * (rows + width) * hidden, transcendentals=0),
        name="result_rows",
    )(hid, second, after)


def widen_kernel(core_ref, half_ref, other_ref, first_ref, second_ref):
    half, other = half_ref[...].astype(f32), other_ref[...].astype(f32)
    swapped = core_ref[0] == 1
    first_ref[0] = jnp.where(swapped, other, half)
    second_ref[0] = jnp.where(swapped, half, other)


def widen(core, half, other):
    hidden, width = half.shape
    cut = width // 2
    rows = pl.BlockSpec((cut, width), lambda s, j, w: (2 * s + j, 0))
    return pl.pallas_call(
        widen_kernel,
        grid_spec=pltpu.PrefetchScalarGridSpec(
            num_scalar_prefetch=1,
            grid=(hidden // width, 2),
            in_specs=[rows, rows],
            out_specs=[
                pl.BlockSpec((1, cut, width), lambda s, j, w: (0, j, s)),
                pl.BlockSpec((1, cut, width), lambda s, j, w: (0, 2 * s + j, 0)),
            ],
        ),
        out_shape=[jax.ShapeDtypeStruct((1, width, hidden), f32), jax.ShapeDtypeStruct((1, hidden, width), f32)],
        compiler_params=pltpu.CompilerParams(vmem_limit_bytes=40 * 2**20),
        name="widen",
    )(core.reshape(1), half, other)


def rms_norm(values_in, gain_vec):
    return (
        values_in
        * lax.rsqrt(jnp.mean(values_in * values_in, axis=-1, keepdims=True) + 1e-06)
        * gain_vec
    )


def log2(n):
    return n.bit_length() - 1


def swap(x, axis, bit):
    n = lax.axis_size(axis)
    return lax.ppermute(x, axis, [(i, i ^ (1 << bit)) for i in range(n)])


def side(axis, bit):
    return (lax.axis_index(axis) >> bit) & 1


def gather_bits(x, axis, dim, order):
    bits = log2(lax.axis_size(axis))
    for bit in order:
        other = swap(x, axis, bit)
        mine = side(axis, bit) == 1
        at = dim + bits - 1 - bit
        x = jnp.concatenate([jnp.where(mine, other, x), jnp.where(mine, x, other)], axis=at)
    return x


def reduce_bits(x, axis, dim, order):
    bits = log2(lax.axis_size(axis))
    for bit in order:
        at = dim + bits - 1 - bit
        mine = side(axis, bit)
        keep = lax.dynamic_index_in_dim(x, mine, at)
        away = lax.dynamic_index_in_dim(x, 1 - mine, at)
        x = (keep.astype(f32) + swap(away, axis, bit).astype(f32)).astype(bf16)
    return x


def paths(axis):
    bits = log2(lax.axis_size(axis))
    rest = list(range(1, bits))
    return rest, rest[::-1]


def across(x, axis, k):
    n = lax.axis_size(axis)
    return lax.ppermute(x, axis, [(i, i ^ k) for i in range(n)])


def around(piece, ring):
    m, me = lax.axis_size(ring), lax.axis_index(ring)
    parts = [piece] + [across(piece, ring, k) for k in range(1, m)]
    for bit in range(log2(m)):
        odd = side(ring, bit) == 1
        parts = [jnp.where(odd, parts[k ^ (1 << bit)], parts[k]) for k in range(m)]
    return jnp.stack(parts)


def spread(held, axis, order):
    n, bits = lax.axis_size(axis), log2(lax.axis_size(axis))
    m, rows, columns = held.shape
    held = held.reshape((m,) + (1,) * bits + (rows, columns))
    held = gather_bits(held, axis, 1, order + [0])
    return held.reshape(m * n * rows, columns)


def add(x, y):
    return (x.astype(f32) + y.astype(f32)).astype(bf16)


def collect(x, axis, ring):
    bits, m = log2(lax.axis_size(axis)) - 1, lax.axis_size(ring)
    rows, columns = x.shape
    x = x.reshape((m, 2) + (2,) * bits + (rows // m // 2 >> bits, columns))
    both = [x[:, 0], x[:, 1]]
    for orders in zip(*paths(axis)):
        both = [reduce_bits(y, axis, 1, [bit]) for y, bit in zip(both, orders)]
    me = lax.axis_index(ring)
    for path in (0, 1):
        total = lax.dynamic_index_in_dim(both[path], me, 0).astype(f32)
        for k in range(1, m):
            total = total + across(lax.dynamic_index_in_dim(both[path], me ^ k, 0), ring, k).astype(f32)
        both[path] = total.astype(bf16)
    for orders in zip(*(order[::-1] for order in paths(axis))):
        both = [gather_bits(y, axis, 1, [bit]) for y, bit in zip(both, orders)]
    return jnp.concatenate([y.reshape(rows // m // 2, columns) for y in both], 0)


def on_device(
    tokens,
    cotangent,
    segments,
    routes,
    w_query,
    w_key,
    w_value,
    w_output,
    norm_attn,
    norm_ffn,
    w_router,
    rel_bias,
    expert_input_weight,
    expert_output_weight,
):
    R, S = "replica", "shard"
    one, two = paths(R)
    rows, width = tokens.shape
    heads = rel_bias.shape[1]
    head = width // heads
    experts = w_router.shape[1]
    owned = w_query.shape[0]
    near = rel_bias.shape[0]
    me = lax.axis_index(S)
    capacity = 5 * rows // (4 * experts)

    replica = lax.axis_index(R)
    few = owned // lax.axis_size(R)

    def mine_of(w):
        return lax.dynamic_slice_in_dim(w, replica * few, few, 0)

    blank = lambda n: jnp.zeros((few, n), bf16)
    bias_rows = mine_of(jnp.pad(rel_bias, ((0, owned - near), (0, 0))))
    extra = [mine_of(norm_attn)[:, None], mine_of(norm_ffn)[:, None], mine_of(w_router), blank(6 - experts), bias_rows, blank(120 - heads)]
    cut = 3 * width // 2
    packed = jnp.concatenate([mine_of(w_query), mine_of(w_key), mine_of(w_value)], axis=1)
    held_one = around(jnp.concatenate([packed[:, :cut]] + extra, 1), S)
    held_two = around(packed[:, cut:], S)
    full_output = lax.all_gather(mine_of(w_output), (S, R), axis=0, tiled=True)
    held_one, held_two, late = lax.optimization_barrier((held_one, held_two, cotangent))
    part_one, part_two = spread(held_one, R, one), spread(held_two, R, two)
    full_qkv = jnp.concatenate([part_one[:, :cut], part_two], axis=1)
    small = part_one[:, cut:]
    gain_one = small[:, 0].astype(f32)
    gain_two = small[:, 1].astype(f32)
    router = small[:, 2 : 2 + experts]
    table = small.reshape(-1, owned, 128)[:, : rel_bias.shape[0], 8 : 8 + heads].reshape(-1, heads)
    buckets = table.shape[0]

    names = me ^ jnp.arange(experts, dtype=jnp.int32)
    chosen = (names[:, None] == routes[:, 0][None, :]).astype(bf16)
    ids = jnp.arange(rows, dtype=jnp.int32)
    earlier = (ids[:, None] < ids[None, :]).astype(bf16)
    slot = jnp.dot(chosen, earlier, preferred_element_type=f32).astype(jnp.int32)
    places = (
        (chosen[:, None, :] == 1)
        & (slot[:, None, :] == jnp.arange(capacity, dtype=jnp.int32)[None, :, None])
    ).astype(bf16)

    def send(values):
        out = [dot(places[k], values).astype(bf16) for k in range(experts)]
        return [out[0]] + [across(out[k], S, k) for k in range(1, experts)]

    def take(back):
        return dot(places.reshape(-1, rows), jnp.concatenate(back, 0), TN)

    g_rows = send(late)

    inputs = tokens.astype(f32)
    normed_one = rms_norm(inputs, gain_one).astype(bf16)
    qkv = lax.dot_general(full_qkv, normed_one, (((0,), (1,)), ((), ())), preferred_element_type=f32)
    qkv = qkv.astype(bf16).reshape(3 * heads, head, rows)
    aug_q, aug_k, line = helpers(segments[0], table)
    e, att, inv = attend(qkv, aug_q, aug_k, line, heads)
    att_t = att.reshape(width, rows)
    middle = inputs + dot(att_t, full_output, TN)
    normed_two = rms_norm(middle, gain_two).astype(bf16)
    x_rows = send(normed_two)

    logits = jnp.dot(normed_two, router, preferred_element_type=f32)
    gate_probs = jax.nn.softmax(logits, axis=-1)
    named = (routes == jnp.arange(experts, dtype=jnp.int32)[None, :]).astype(f32)
    chosen_gate = jnp.sum(gate_probs * named, axis=-1)

    router_wide = jnp.pad(router, ((0, 0), (0, 128 - experts)))
    mine = jnp.broadcast_to((jnp.arange(128) == me).astype(f32)[None], (8, 128))
    kept, backs, logs = (), [], []
    for k in range(experts):
        *kept, back, log = expert_pass(
            k, experts, x_rows[k], g_rows[k], expert_input_weight, expert_output_weight,
            router_wide, mine, kept, backs[k - 2 : k - 1] if k > 2 else [], experts,
        )
        backs.append(across(back, S, k) if k else back)
        logs.append(log)
    hid, pre, xs, gs = kept
    core = side(R, 0)
    away = weight_half(1 - core, hid, pre, xs, gs, backs[-2])
    swapped = swap(away, R, 0)
    keep = weight_half(core, hid, pre, xs, gs, backs[-1])
    half = (keep.astype(f32) + swapped.astype(f32)).astype(bf16).reshape(-1, width)
    half_sum = half
    groups = [list(range(j, lax.axis_size(R), 2)) for j in (0, 1)]
    part = lax.psum_scatter(half, R, scatter_dimension=0, tiled=True, axis_index_groups=groups)
    half = lax.all_gather(part, R, axis=0, tiled=True, axis_index_groups=groups)
    total_first, total_second = widen(core, half, swap(half, R, 0))
    xs_flat = xs.reshape(-1, width)
    grad_normed_two = take(backs)
    grad_router = dot(xs_flat, jnp.concatenate(logs, 0).astype(bf16), TN)[:, :experts]

    grad_final = cotangent.astype(f32)
    grad_mid_norm, grad_gain_two = jax.vjp(rms_norm, middle, gain_two)[1](grad_normed_two)
    grad_middle = grad_final + grad_mid_norm
    grad_branch = grad_middle.astype(bf16)
    mid = width // 2

    def halves(make, count):
        return make(core * count), make((1 - core) * count)

    out_keep, out_away = halves(
        lambda at: dot(att_t, lax.dynamic_slice_in_dim(grad_branch, at, mid, 1)).astype(bf16), mid
    )
    grad_att = dot(full_output, grad_branch, NT).astype(bf16).reshape(heads, head, rows)
    results = [result_rows(k, hid, expert_output_weight, backs[-1]) for k in range(experts)]
    dots = results
    results = [results[0]] + [across(results[k], S, k) for k in range(1, experts)]
    mixed = (middle + chosen_gate[:, None] * take(results)).astype(bf16)
    out_sum = add(out_keep, swap(out_away, R, 0))
    grad_qkv, diag, far = pull(e, grad_att, att, inv, qkv, heads, [half_sum] + dots)
    grad_qkv = grad_qkv.reshape(3 * width, rows)
    grad_table = table_grad(diag, far, buckets)
    half_dims = (((0,), (1,)), ((), ()))
    qkv_keep, qkv_away = halves(
        lambda at: dot(normed_one, lax.dynamic_slice_in_dim(grad_qkv, at, cut, 0), half_dims).astype(bf16), cut
    )
    grad_normed_one = lax.dot_general(
        grad_qkv, full_qkv, (((0,), (1,)), ((), ())), preferred_element_type=f32
    )
    grad_in_norm, grad_gain_one = jax.vjp(rms_norm, inputs, gain_one)[1](grad_normed_one)
    grad_inputs = grad_middle + grad_in_norm

    table_rows = jnp.pad(grad_table.reshape(-1, near, heads), ((0, 0), (0, owned - near), (0, 0))).reshape(width, heads)
    rest = jnp.concatenate(
        [grad_gain_one[:, None], grad_gain_two[:, None], grad_router, jnp.zeros((width, 6 - experts), f32), table_rows, jnp.zeros((width, 120 - heads), f32)], 1
    ).astype(bf16)
    qkv_sum = add(qkv_keep, swap(qkv_away, R, 0))
    rest_sum = add(rest, swap(rest, R, 0))
    sums = collect(jnp.concatenate([qkv_sum, out_sum, rest_sum], 1), R, S)
    both_sums = sums[:, : cut + mid]
    other_sums = swap(both_sums, R, 0)
    sum_rest = sums[:, cut + mid :]

    def ordered(keep, away):
        return jnp.concatenate([jnp.where(core == 0, keep, away), jnp.where(core == 0, away, keep)], 1).astype(f32)

    sum_qkv, sum_out = ordered(both_sums[:, :cut], other_sums[:, :cut]), ordered(both_sums[:, cut:], other_sums[:, cut:])
    sum_rest = sum_rest.astype(f32)
    return (
        mixed,
        grad_inputs,
        sum_qkv[:, :width],
        sum_qkv[:, width : 2 * width],
        sum_qkv[:, 2 * width :],
        sum_out,
        sum_rest[:, 0],
        sum_rest[:, 1],
        sum_rest[:, 2 : 2 + experts],
        sum_rest[:near, 8 : 8 + heads],
        total_first,
        total_second,
    )


def solution(mesh):
    rows = P(("replica", "shard"), None)
    own, vec, cube = P("shard", None), P("shard"), P("shard", None, None)
    return jax.shard_map(
        on_device,
        mesh=mesh,
        in_specs=(rows,) * 4 + (own,) * 4 + (vec,) * 2 + (own,) * 2 + (cube,) * 2,
        out_specs=(rows,) * 2 + (own,) * 4 + (vec,) * 2 + (own,) * 2 + (cube,) * 2,
        check_vma=False,
    )
```

```python
from functools import partial
import jax, jax.numpy as jnp
from jax import lax
from jax.experimental import pallas as pl
from jax.experimental.pallas import tpu as pltpu
from jax.sharding import PartitionSpec as P

f32, bf16 = jnp.float32, jnp.bfloat16
NN = (((1,), (0,)), ((), ()))
NT = (((1,), (1,)), ((), ()))
TN = (((0,), (0,)), ((), ()))
ROOT = 0.7978845608028654
CUBE = 0.044715


def dot(a, b, dims=NN):
    return lax.dot_general(a, b, dims, preferred_element_type=f32)


def attend_kernel(q_ref, k_ref, v_ref, aug_q_ref, aug_k_ref, line_ref, e_ref, att_ref, inv_ref, s_ref, k_nat, rows=256, cols=256):
    length = k_ref.shape[-1]
    band = 128
    k_nat[...] = jnp.concatenate([k_ref[0], aug_k_ref[...]], axis=0).T
    q_aug = jnp.concatenate([q_ref[0], aug_q_ref[0]], axis=0)
    v_aug = jnp.concatenate([v_ref[0], jnp.ones((16, length), bf16)], axis=0)
    line = jnp.broadcast_to(line_ref[0, 0:1, :], (band, 4 * band))
    skew = pltpu.roll(line, 0, 1, stride=1, stride_axis=0)
    near = [skew[:, (2 - o) * band : (3 - o) * band] for o in (-1, 0, 1)]
    width = v_ref.shape[1]
    for c in range(0, length, cols):
        top = None
        for r in range(0, length, rows):
            s = dot(k_nat[r : r + rows, :], q_aug[:, c : c + cols])
            pieces = []
            for i in range(r // band, (r + rows) // band):
                blocks = []
                for j in range(c // band, (c + cols) // band):
                    blk = s[i * band - r : (i + 1) * band - r, j * band - c : (j + 1) * band - c]
                    if abs(i - j) <= 1:
                        blk = blk + near[i - j + 1]
                    blocks.append(blk)
                pieces.append(jnp.concatenate(blocks, axis=1))
            s = jnp.concatenate(pieces, axis=0)
            s_ref[r : r + rows, :] = s
            m = jnp.max(s.reshape(rows // 8, 8, cols), axis=0)
            top = m if top is None else jnp.maximum(top, m)
        top = jnp.max(top, axis=0, keepdims=True)
        out = None
        for r in range(0, length, rows):
            e = jnp.exp(s_ref[r : r + rows, :] - top).astype(bf16)
            e_ref[0, r : r + rows, c : c + cols] = e
            part = dot(v_aug[:, r : r + rows], e)
            out = part if out is None else out + part
        inv = 1.0 / out[width : width + 1, :]
        inv_ref[0, :, c : c + cols] = jnp.broadcast_to(inv, (8, cols))
        att_ref[0, :, c : c + cols] = (out[:width] * inv).astype(bf16)


def attend(qkv, aug_q, aug_k, line, heads):
    width, length = qkv.shape[1:]
    head = lambda off: pl.BlockSpec((1, width, length), lambda h: (h + off, 0, 0))
    return pl.pallas_call(
        attend_kernel,
        grid=(heads,),
        in_specs=[head(0), head(heads), head(2 * heads),
                  pl.BlockSpec((1, 16, length), lambda h: (h, 0, 0)),
                  pl.BlockSpec((16, length), lambda h: (0, 0)),
                  pl.BlockSpec((1, 8, 512), lambda h: (h, 0, 0))],
        out_specs=[pl.BlockSpec((1, length, length), lambda h: (h, 0, 0)),
                   pl.BlockSpec((1, width, length), lambda h: (h, 0, 0)),
                   pl.BlockSpec((1, 8, length), lambda h: (h, 0, 0))],
        out_shape=[jax.ShapeDtypeStruct((heads, length, length), bf16),
                   jax.ShapeDtypeStruct((heads, width, length), bf16),
                   jax.ShapeDtypeStruct((heads, 8, length), f32)],
        scratch_shapes=[pltpu.VMEM((length, 256), f32), pltpu.VMEM((length, width + 16), bf16)],
        compiler_params=pltpu.CompilerParams(vmem_limit_bytes=40 * 2**20),
        cost_estimate=pl.CostEstimate(flops=heads * length * length * 256 * 4, bytes_accessed=heads * length * length * 2, transcendentals=heads * length * length),
        name="attend",
    )(qkv, qkv, qkv, aug_q, aug_k, line)


def pull_kernel(e_ref, g_ref, att_ref, inv_ref, q_ref, k_ref, v_ref, *rest, rows=256, cols=256):
    grad_ref, diag_ref, far_ref, v_nat, gs_ref, near_ref = rest[-6:]
    length = k_ref.shape[-1]
    band = 128
    g = (g_ref[0].astype(f32) * inv_ref[0, 0:1, :]).astype(bf16)
    delta = jnp.sum(g.astype(f32) * att_ref[0].astype(f32), axis=0, keepdims=True)
    hi = delta.astype(bf16)
    lo = (delta - hi.astype(f32)).astype(bf16)
    pad = jnp.concatenate([hi.astype(f32), lo.astype(f32), jnp.zeros((14, length), f32)], axis=0)
    g_aug = jnp.concatenate([g, (-pad).astype(bf16)], axis=0)
    v_nat[...] = jnp.concatenate([v_ref[0], jnp.ones((16, length), bf16)], axis=0).T
    near_ref[...] = jnp.zeros_like(near_ref)
    far = [jnp.zeros((8, band), f32), jnp.zeros((8, band), f32)]
    for c in range(0, length, cols):
        for r in range(0, length, rows):
            gp = dot(v_nat[r : r + rows, :], g_aug[:, c : c + cols])
            gs = e_ref[0, r : r + rows, c : c + cols].astype(f32) * gp
            gs_ref[r : r + rows, c : c + cols] = gs.astype(bf16)
            for i in range(r // band, (r + rows) // band):
                for j in range(c // band, (c + cols) // band):
                    blk = gs[i * band - r : (i + 1) * band - r, j * band - c : (j + 1) * band - c]
                    if abs(i - j) <= 1:
                        lane = (2 - (i - j)) * band
                        near_ref[:, lane : lane + band] += blk
                    else:
                        side = int(i > j)
                        far[side] = far[side] + jnp.sum(blk.reshape(band // 8, 8, band), axis=0)
    skew = near_ref[0:8, :]
    for a in range(8, band, 8):
        skew = skew + pltpu.roll(near_ref[a : a + 8, :], 4 * band - a, 1)
    diag_ref[0] = skew
    far_ref[0] = jnp.concatenate(far, axis=1)
    grad_ref[2, 0] = dot(g, e_ref[0], NT).astype(bf16)
    grad_ref[1, 0] = dot(q_ref[0], gs_ref[...], NT).astype(bf16)
    grad_ref[0, 0] = dot(k_ref[0], gs_ref[...]).astype(bf16)


def pull(e, g, att, inv, qkv, heads, after):
    width, length = qkv.shape[1:]
    head = lambda off: pl.BlockSpec((1, width, length), lambda h: (h + off, 0, 0))
    return pl.pallas_call(
        pull_kernel,
        grid=(heads,),
        in_specs=[pl.BlockSpec((1, length, length), lambda h: (h, 0, 0)), head(0), head(0),
                  pl.BlockSpec((1, 8, length), lambda h: (h, 0, 0)), head(0), head(heads), head(2 * heads)]
        + [pl.BlockSpec(memory_space=pl.ANY)] * len(after),
        out_specs=[pl.BlockSpec((3, 1, width, length), lambda h: (0, h, 0, 0)),
                   pl.BlockSpec((1, 8, 512), lambda h: (h, 0, 0)),
                   pl.BlockSpec((1, 8, 256), lambda h: (h, 0, 0))],
        out_shape=[jax.ShapeDtypeStruct((3, heads, width, length), bf16), jax.ShapeDtypeStruct((heads, 8, 512), f32), jax.ShapeDtypeStruct((heads, 8, 256), f32)],
        scratch_shapes=[pltpu.VMEM((length, width + 16), bf16), pltpu.VMEM((length, length), bf16), pltpu.VMEM((128, 512), f32)],
        compiler_params=pltpu.CompilerParams(vmem_limit_bytes=40 * 2**20),
        cost_estimate=pl.CostEstimate(flops=heads * length * length * 256 * 8, bytes_accessed=heads * length * length * 2, transcendentals=0),
        name="pull",
    )(e, g, att, inv, qkv, qkv, qkv, *after)


def bucket_of(r):
    n = jnp.abs(r)
    far = sum((n >= t).astype(jnp.int32) for t in (12, 16, 23, 32, 46, 64, 91))
    return jnp.where(n < 8, n, 8 + far) + 16 * (r > 0)


def helpers(segments, rel_bias):
    length = segments.shape[0]
    heads = rel_bias.shape[1]
    seg = (segments[None, :] == jnp.arange(4)[:, None]).astype(f32)
    blk = jnp.arange(length) // 128
    nb = length // 128
    own = (blk[None, :] == jnp.arange(nb)[:, None]).astype(f32)
    aug_k = jnp.concatenate([seg, own, jnp.zeros((12 - nb, length), f32)], 0).astype(bf16)
    left, right = rel_bias[15], rel_bias[31]
    kb = jnp.arange(nb)[:, None]
    c = jnp.where(kb < blk[None] - 1, left[:, None, None], jnp.where(kb > blk[None] + 1, right[:, None, None], 0))
    aug_q = jnp.concatenate([jnp.broadcast_to(-1e30 * (1 - seg), (heads, 4, length)), c.astype(f32), jnp.zeros((heads, 12 - nb, length), f32)], 1).astype(bf16)
    y = jnp.arange(512)
    hot = (bucket_of(-(y - 256))[None] == jnp.arange(rel_bias.shape[0])[:, None])
    line = jnp.einsum("bh,by->hy", rel_bias, hot.astype(bf16), preferred_element_type=f32)
    return aug_q, aug_k, jnp.broadcast_to(line[:, None], (heads, 8, 512))


def table_grad(diag, far, buckets):
    place = jnp.arange(512)[None, :] - jnp.arange(8)[:, None]
    hot = bucket_of(256 - place)[None] == jnp.arange(buckets)[:, None, None]
    t = jnp.einsum("kby,hby->kh", hot.astype(f32), diag, precision=lax.Precision.HIGHEST)
    l = jnp.sum(far[:, :, :128], (1, 2)); r = jnp.sum(far[:, :, 128:], (1, 2))
    b = jnp.arange(buckets)[:, None]
    return t + jnp.where(b == 15, l, 0) + jnp.where(b == 31, r, 0)


def expert_kernel(x_ref, g_ref, first_ref, second_ref, router_ref, mine_ref, *rest, experts):
    hid_ref, pre_ref, xs_ref, gs_ref, back_ref, log_ref, acc_ref, prob_ref, dot_ref = rest[-9:]
    step, last = pl.program_id(0), pl.num_programs(0) - 1
    x, g = x_ref[...], g_ref[...]

    @pl.when(step == 0)
    def _():
        lane = lax.broadcasted_iota(jnp.int32, prob_ref.shape, 1)
        logits = jnp.where(lane < experts, dot(x, router_ref[...]), -1e30)
        shifted = jnp.exp(logits - jnp.max(logits, axis=1, keepdims=True))
        prob_ref[...] = shifted / jnp.sum(shifted, axis=1, keepdims=True)
        acc_ref[...] = jnp.zeros_like(acc_ref)
        dot_ref[...] = jnp.zeros_like(dot_ref)

    gate = jnp.sum(prob_ref[...] * mine_ref[0:1, :], axis=1, keepdims=True)
    u = dot(x, first_ref[0])
    raw = dot(g, second_ref[0], NT)
    square = u * u
    t = jnp.tanh(u * (ROOT + (ROOT * CUBE) * square))
    half = 0.5 + 0.5 * t
    hidden = (u * half).astype(bf16)
    slope = half + (0.5 * u) * (1.0 - t * t) * (ROOT + (3.0 * ROOT * CUBE) * square)
    grad = (raw * gate * slope).astype(bf16)
    hid_ref[0] = hidden
    pre_ref[0] = grad
    paired = hidden.astype(f32) * raw
    total = dot_ref[...]
    for c in range(0, paired.shape[1], 128):
        total = total + paired[:, c : c + 128]
    dot_ref[...] = total
    acc_ref[...] += dot(grad, first_ref[0], NT)

    @pl.when(step == last)
    def _():
        probs = prob_ref[...]
        pull = jnp.sum(dot_ref[...], axis=1, keepdims=True)
        coming = mine_ref[0:1, :] * pull
        grad_logits = probs * (coming - jnp.sum(probs * coming, axis=1, keepdims=True))
        log_ref[...] = grad_logits
        high = grad_logits.astype(bf16)
        low = (grad_logits - high.astype(f32)).astype(bf16)
        more = dot(high, router_ref[...], NT) + dot(low, router_ref[...], NT)
        back_ref[...] = (acc_ref[...] + more).astype(bf16)
        xs_ref[0] = x
        gs_ref[0] = (g.astype(f32) * gate).astype(bf16)


def expert_pass(turn, turns, x, g, first, second, router, mine, kept, after, experts):
    rows, width = x.shape
    hidden = first.shape[2]
    cut = 512 if hidden % 512 == 0 else hidden
    whole = lambda *shape: pl.BlockSpec(shape, lambda s: (0,) * len(shape))
    hold = pl.BlockSpec((1, rows, cut), lambda s: (turn, 0, s))
    row = pl.BlockSpec((1, rows, width), lambda s: (turn, 0, 0))
    struct = jax.ShapeDtypeStruct
    return pl.pallas_call(
        partial(expert_kernel, experts=experts),
        grid=(hidden // cut,),
        in_specs=[
            whole(rows, width),
            whole(rows, width),
            pl.BlockSpec((1, width, cut), lambda s: (0, 0, s)),
            pl.BlockSpec((1, cut, width), lambda s: (0, s, 0)),
            whole(width, 128),
            whole(8, 128),
        ]
        + [pl.BlockSpec(memory_space=pl.ANY)] * (len(kept) + len(after)),
        out_specs=[hold, hold, row, row, whole(rows, width), whole(rows, 128)],
        out_shape=[
            struct((turns, rows, hidden), bf16),
            struct((turns, rows, hidden), bf16),
            struct((turns, rows, width), bf16),
            struct((turns, rows, width), bf16),
            struct((rows, width), bf16),
            struct((rows, 128), f32),
        ],
        scratch_shapes=[
            pltpu.VMEM((rows, width), f32),
            pltpu.VMEM((rows, 128), f32),
            pltpu.VMEM((rows, 128), f32),
        ],
        input_output_aliases={6 + i: i for i in range(len(kept))},
        compiler_params=pltpu.CompilerParams(vmem_limit_bytes=40 * 2**20),
        cost_estimate=pl.CostEstimate(
            flops=6 * rows * width * hidden,
            bytes_accessed=4 * width * hidden + 4 * rows * hidden,
            transcendentals=rows * hidden,
        ),
        name="expert_pass",
    )(x, g, first, second, router, mine, *kept, *after)


def weight_half_kernel(which_ref, hid_ref, pre_ref, xs_ref, gs_ref, after_ref, out_ref):
    @pl.when(which_ref[0] == 0)
    def _():
        out_ref[0] = dot(xs_ref[...], pre_ref[...], TN).astype(bf16)

    @pl.when(which_ref[0] == 1)
    def _():
        out_ref[0] = dot(hid_ref[...], gs_ref[...], TN).astype(bf16)


def weight_half(which, hid, pre, xs, gs, after):
    width, hidden = xs.shape[2], hid.shape[2]
    hid, pre, xs, gs = (v.reshape(-1, v.shape[2]) for v in (hid, pre, xs, gs))
    rows, parts = xs.shape[0], hidden // width
    return pl.pallas_call(
        weight_half_kernel,
        grid_spec=pltpu.PrefetchScalarGridSpec(
            num_scalar_prefetch=1,
            grid=(parts,),
            in_specs=[
                pl.BlockSpec((rows, width), lambda s, w: (0, s * w[0])),
                pl.BlockSpec((rows, width), lambda s, w: (0, s * (1 - w[0]))),
                pl.BlockSpec((rows, width), lambda s, w: (0, 0)),
                pl.BlockSpec((rows, width), lambda s, w: (0, 0)),
                pl.BlockSpec(memory_space=pl.ANY),
            ],
            out_specs=pl.BlockSpec((1, width, width), lambda s, w: (s, 0, 0)),
        ),
        out_shape=jax.ShapeDtypeStruct((parts, width, width), bf16),
        compiler_params=pltpu.CompilerParams(vmem_limit_bytes=40 * 2**20),
        cost_estimate=pl.CostEstimate(flops=2 * rows * width * hidden, bytes_accessed=2 * (rows + width) * hidden, transcendentals=0),
        name="weight_half",
    )(which.reshape(1), hid, pre, xs, gs, after)


def result_kernel(hid_ref, second_ref, after_ref, out_ref):
    out_ref[...] = dot(hid_ref[0], second_ref[0]).astype(bf16)


def result_rows(turn, hid, second, after):
    rows, hidden, width = hid.shape[1], hid.shape[2], second.shape[2]
    return pl.pallas_call(
        result_kernel,
        grid=(1,),
        in_specs=[
            pl.BlockSpec((1, rows, hidden), lambda s: (turn, 0, 0)),
            pl.BlockSpec((1, hidden, width), lambda s: (0, 0, 0)),
            pl.BlockSpec(memory_space=pl.ANY),
        ],
        out_specs=pl.BlockSpec((rows, width), lambda s: (0, 0)),
        out_shape=jax.ShapeDtypeStruct((rows, width), bf16),
        compiler_params=pltpu.CompilerParams(vmem_limit_bytes=40 * 2**20),
        cost_estimate=pl.CostEstimate(flops=2 * rows * width * hidden, bytes_accessed=2 * (rows + width) * hidden, transcendentals=0),
        name="result_rows",
    )(hid, second, after)


def widen_kernel(core_ref, half_ref, other_ref, first_ref, second_ref):
    half, other = half_ref[...].astype(f32), other_ref[...].astype(f32)
    swapped = core_ref[0] == 1
    first_ref[0] = jnp.where(swapped, other, half)
    second_ref[0] = jnp.where(swapped, half, other)


def widen(core, half, other):
    hidden, width = half.shape
    cut = width // 2
    rows = pl.BlockSpec((cut, width), lambda s, j, w: (2 * s + j, 0))
    return pl.pallas_call(
        widen_kernel,
        grid_spec=pltpu.PrefetchScalarGridSpec(
            num_scalar_prefetch=1,
            grid=(hidden // width, 2),
            in_specs=[rows, rows],
            out_specs=[
                pl.BlockSpec((1, cut, width), lambda s, j, w: (0, j, s)),
                pl.BlockSpec((1, cut, width), lambda s, j, w: (0, 2 * s + j, 0)),
            ],
        ),
        out_shape=[jax.ShapeDtypeStruct((1, width, hidden), f32), jax.ShapeDtypeStruct((1, hidden, width), f32)],
        compiler_params=pltpu.CompilerParams(vmem_limit_bytes=40 * 2**20),
        name="widen",
    )(core.reshape(1), half, other)


def rms_norm(values_in, gain_vec):
    return (
        values_in
        * lax.rsqrt(jnp.mean(values_in * values_in, axis=-1, keepdims=True) + 1e-06)
        * gain_vec
    )


def log2(n):
    return n.bit_length() - 1


def swap(x, axis, bit):
    n = lax.axis_size(axis)
    return lax.ppermute(x, axis, [(i, i ^ (1 << bit)) for i in range(n)])


def side(axis, bit):
    return (lax.axis_index(axis) >> bit) & 1


def gather_bits(x, axis, dim, order):
    bits = log2(lax.axis_size(axis))
    for bit in order:
        other = swap(x, axis, bit)
        mine = side(axis, bit) == 1
        at = dim + bits - 1 - bit
        x = jnp.concatenate([jnp.where(mine, other, x), jnp.where(mine, x, other)], axis=at)
    return x


def reduce_bits(x, axis, dim, order):
    bits = log2(lax.axis_size(axis))
    for bit in order:
        at = dim + bits - 1 - bit
        mine = side(axis, bit)
        keep = lax.dynamic_index_in_dim(x, mine, at)
        away = lax.dynamic_index_in_dim(x, 1 - mine, at)
        x = (keep.astype(f32) + swap(away, axis, bit).astype(f32)).astype(bf16)
    return x


def paths(axis):
    bits = log2(lax.axis_size(axis))
    rest = list(range(1, bits))
    return rest, rest[::-1]


def across(x, axis, k):
    n = lax.axis_size(axis)
    return lax.ppermute(x, axis, [(i, i ^ k) for i in range(n)])


def around(piece, ring):
    m, me = lax.axis_size(ring), lax.axis_index(ring)
    parts = [piece] + [across(piece, ring, k) for k in range(1, m)]
    for bit in range(log2(m)):
        odd = side(ring, bit) == 1
        parts = [jnp.where(odd, parts[k ^ (1 << bit)], parts[k]) for k in range(m)]
    return jnp.stack(parts)


def spread(held, axis, order):
    n, bits = lax.axis_size(axis), log2(lax.axis_size(axis))
    m, rows, columns = held.shape
    held = held.reshape((m,) + (1,) * bits + (rows, columns))
    held = gather_bits(held, axis, 1, order + [0])
    return held.reshape(m * n * rows, columns)


def add(x, y):
    return (x.astype(f32) + y.astype(f32)).astype(bf16)


def collect(x, axis, ring):
    bits, m = log2(lax.axis_size(axis)) - 1, lax.axis_size(ring)
    rows, columns = x.shape
    x = x.reshape((m, 2) + (2,) * bits + (rows // m // 2 >> bits, columns))
    both = [x[:, 0], x[:, 1]]
    for orders in zip(*paths(axis)):
        both = [reduce_bits(y, axis, 1, [bit]) for y, bit in zip(both, orders)]
    me = lax.axis_index(ring)
    for path in (0, 1):
        total = lax.dynamic_index_in_dim(both[path], me, 0).astype(f32)
        for k in range(1, m):
            total = total + across(lax.dynamic_index_in_dim(both[path], me ^ k, 0), ring, k).astype(f32)
        both[path] = total.astype(bf16)
    for orders in zip(*(order[::-1] for order in paths(axis))):
        both = [gather_bits(y, axis, 1, [bit]) for y, bit in zip(both, orders)]
    return jnp.concatenate([y.reshape(rows // m // 2, columns) for y in both], 0)


def on_device(
    tokens,
    cotangent,
    segments,
    routes,
    w_query,
    w_key,
    w_value,
    w_output,
    norm_attn,
    norm_ffn,
    w_router,
    rel_bias,
    expert_input_weight,
    expert_output_weight,
):
    R, S = "replica", "shard"
    one, two = paths(R)
    rows, width = tokens.shape
    heads = rel_bias.shape[1]
    head = width // heads
    experts = w_router.shape[1]
    owned = w_query.shape[0]
    near = rel_bias.shape[0]
    me = lax.axis_index(S)
    capacity = 5 * rows // (4 * experts)

    replica = lax.axis_index(R)
    few = owned // lax.axis_size(R)

    def mine_of(w):
        return lax.dynamic_slice_in_dim(w, replica * few, few, 0)

    blank = lambda n: jnp.zeros((few, n), bf16)
    bias_rows = mine_of(jnp.pad(rel_bias, ((0, owned - near), (0, 0))))
    extra = [mine_of(norm_attn)[:, None], mine_of(norm_ffn)[:, None], mine_of(w_router), blank(6 - experts), bias_rows, blank(120 - heads)]
    cut = 3 * width // 2
    packed = jnp.concatenate([mine_of(w_query), mine_of(w_key), mine_of(w_value)], axis=1)
    held_one = around(jnp.concatenate([packed[:, :cut]] + extra, 1), S)
    held_two = around(packed[:, cut:], S)
    full_output = lax.all_gather(mine_of(w_output), (S, R), axis=0, tiled=True)
    held_one, held_two, late = lax.optimization_barrier((held_one, held_two, cotangent))
    part_one, part_two = spread(held_one, R, one), spread(held_two, R, two)
    full_qkv = jnp.concatenate([part_one[:, :cut], part_two], axis=1)
    small = part_one[:, cut:]
    gain_one = small[:, 0].astype(f32)
    gain_two = small[:, 1].astype(f32)
    router = small[:, 2 : 2 + experts]
    table = small.reshape(-1, owned, 128)[:, : rel_bias.shape[0], 8 : 8 + heads].reshape(-1, heads)
    buckets = table.shape[0]

    names = me ^ jnp.arange(experts, dtype=jnp.int32)
    chosen = (names[:, None] == routes[:, 0][None, :]).astype(bf16)
    ids = jnp.arange(rows, dtype=jnp.int32)
    earlier = (ids[:, None] < ids[None, :]).astype(bf16)
    slot = jnp.dot(chosen, earlier, preferred_element_type=f32).astype(jnp.int32)
    places = (
        (chosen[:, None, :] == 1)
        & (slot[:, None, :] == jnp.arange(capacity, dtype=jnp.int32)[None, :, None])
    ).astype(bf16)

    def send(values):
        out = [dot(places[k], values).astype(bf16) for k in range(experts)]
        return [out[0]] + [across(out[k], S, k) for k in range(1, experts)]

    def take(back):
        return dot(places.reshape(-1, rows), jnp.concatenate(back, 0), TN)

    g_rows = send(late)

    inputs = tokens.astype(f32)
    normed_one = rms_norm(inputs, gain_one).astype(bf16)
    qkv = lax.dot_general(full_qkv, normed_one, (((0,), (1,)), ((), ())), preferred_element_type=f32)
    qkv = qkv.astype(bf16).reshape(3 * heads, head, rows)
    aug_q, aug_k, line = helpers(segments[0], table)
    e, att, inv = attend(qkv, aug_q, aug_k, line, heads)
    att_t = att.reshape(width, rows)
    middle = inputs + dot(att_t, full_output, TN)
    normed_two = rms_norm(middle, gain_two).astype(bf16)
    x_rows = send(normed_two)

    logits = jnp.dot(normed_two, router, preferred_element_type=f32)
    gate_probs = jax.nn.softmax(logits, axis=-1)
    named = (routes == jnp.arange(experts, dtype=jnp.int32)[None, :]).astype(f32)
    chosen_gate = jnp.sum(gate_probs * named, axis=-1)

    router_wide = jnp.pad(router, ((0, 0), (0, 128 - experts)))
    mine = jnp.broadcast_to((jnp.arange(128) == me).astype(f32)[None], (8, 128))
    kept, backs, logs = (), [], []
    for k in range(experts):
        *kept, back, log = expert_pass(
            k, experts, x_rows[k], g_rows[k], expert_input_weight, expert_output_weight,
            router_wide, mine, kept, backs[k - 2 : k - 1] if k > 2 else [], experts,
        )
        backs.append(across(back, S, k) if k else back)
        logs.append(log)
    hid, pre, xs, gs = kept
    core = side(R, 0)
    away = weight_half(1 - core, hid, pre, xs, gs, backs[-2])
    swapped = swap(away, R, 0)
    keep = weight_half(core, hid, pre, xs, gs, backs[-2])
    half = (keep.astype(f32) + swapped.astype(f32)).astype(bf16).reshape(-1, width)
    half_sum = half
    groups = [list(range(j, lax.axis_size(R), 2)) for j in (0, 1)]
    part = lax.psum_scatter(half, R, scatter_dimension=0, tiled=True, axis_index_groups=groups)
    half = lax.all_gather(part, R, axis=0, tiled=True, axis_index_groups=groups)
    total_first, total_second = widen(core, half, swap(half, R, 0))
    xs_flat = xs.reshape(-1, width)
    grad_normed_two = take(backs)
    grad_router = dot(xs_flat, jnp.concatenate(logs, 0).astype(bf16), TN)[:, :experts]

    grad_final = cotangent.astype(f32)
    grad_mid_norm, grad_gain_two = jax.vjp(rms_norm, middle, gain_two)[1](grad_normed_two)
    grad_middle = grad_final + grad_mid_norm
    grad_branch = grad_middle.astype(bf16)
    mid = width // 2

    def halves(make, count):
        return make(core * count), make((1 - core) * count)

    out_keep, out_away = halves(
        lambda at: dot(att_t, lax.dynamic_slice_in_dim(grad_branch, at, mid, 1)).astype(bf16), mid
    )
    grad_att = dot(full_output, grad_branch, NT).astype(bf16).reshape(heads, head, rows)
    results = [result_rows(k, hid, expert_output_weight, backs[-1]) for k in range(experts)]
    dots = results
    results = [results[0]] + [across(results[k], S, k) for k in range(1, experts)]
    mixed = (middle + chosen_gate[:, None] * take(results)).astype(bf16)
    out_sum = add(out_keep, swap(out_away, R, 0))
    grad_qkv, diag, far = pull(e, grad_att, att, inv, qkv, heads, [half_sum] + dots)
    grad_qkv = grad_qkv.reshape(3 * width, rows)
    grad_table = table_grad(diag, far, buckets)
    half_dims = (((0,), (1,)), ((), ()))
    qkv_keep, qkv_away = halves(
        lambda at: dot(normed_one, lax.dynamic_slice_in_dim(grad_qkv, at, cut, 0), half_dims).astype(bf16), cut
    )
    grad_normed_one = lax.dot_general(
        grad_qkv, full_qkv, (((0,), (1,)), ((), ())), preferred_element_type=f32
    )
    grad_in_norm, grad_gain_one = jax.vjp(rms_norm, inputs, gain_one)[1](grad_normed_one)
    grad_inputs = grad_middle + grad_in_norm

    table_rows = jnp.pad(grad_table.reshape(-1, near, heads), ((0, 0), (0, owned - near), (0, 0))).reshape(width, heads)
    rest = jnp.concatenate(
        [grad_gain_one[:, None], grad_gain_two[:, None], grad_router, jnp.zeros((width, 6 - experts), f32), table_rows, jnp.zeros((width, 120 - heads), f32)], 1
    ).astype(bf16)
    qkv_sum = add(qkv_keep, swap(qkv_away, R, 0))
    rest_sum = add(rest, swap(rest, R, 0))
    sums = collect(jnp.concatenate([qkv_sum, out_sum, rest_sum], 1), R, S)
    both_sums = sums[:, : cut + mid]
    other_sums = swap(both_sums, R, 0)
    sum_rest = sums[:, cut + mid :]

    def ordered(keep, away):
        return jnp.concatenate([jnp.where(core == 0, keep, away), jnp.where(core == 0, away, keep)], 1).astype(f32)

    sum_qkv, sum_out = ordered(both_sums[:, :cut], other_sums[:, :cut]), ordered(both_sums[:, cut:], other_sums[:, cut:])
    sum_rest = sum_rest.astype(f32)
    return (
        mixed,
        grad_inputs,
        sum_qkv[:, :width],
        sum_qkv[:, width : 2 * width],
        sum_qkv[:, 2 * width :],
        sum_out,
        sum_rest[:, 0],
        sum_rest[:, 1],
        sum_rest[:, 2 : 2 + experts],
        sum_rest[:near, 8 : 8 + heads],
        total_first,
        total_second,
    )


def solution(mesh):
    rows = P(("replica", "shard"), None)
    own, vec, cube = P("shard", None), P("shard"), P("shard", None, None)
    return jax.shard_map(
        on_device,
        mesh=mesh,
        in_specs=(rows,) * 4 + (own,) * 4 + (vec,) * 2 + (own,) * 2 + (cube,) * 2,
        out_specs=(rows,) * 2 + (own,) * 4 + (vec,) * 2 + (own,) * 2 + (cube,) * 2,
        check_vma=False,
    )
```
